128 devices in a mesh: grid: 128 (over y, z, x, core).
Axes of the slice: x: 4, y: 4, z: 4, core: 2. Of those that a mesh axis runs over, the one named last changes fastest.
Arguments:
- density_blocks: float32 [512, 12, 128, 128], P('grid'), may hold values from -0.15625 to 0.15625
- block_cols: int32 [512, 12], P('grid'), may hold values from 0 to 511, as said below
Outputs:
- purified: float32 [512, 12, 128, 128], P('grid')
The draws below stay inside these ranges and needn't reach their ends.
Inputs may be any that keep to these rules, and one draw needn't show every extreme that they name: `block_cols`: each block row holds 12 distinct block column indices in increasing order, among them its own index, all within 3 * 4 of it.
All inputs are finite; a program needn't handle non-finite values.
Results may differ from the reference program's by a relative error of at most 0.0003.
Values sent between devices are 32-bit elements; how exact they have to be, the bound alone decides.
A program may use at most 192 MiB of HBM per device.

```python
import jax
import jax.numpy as jnp
from jax import lax

BS = 128
NNZ = 12
NEAR = 3
RB_DEV = 4
NBR = 512


def draw_block_cols(key, part):
    key = jax.random.fold_in(key, 7)
    half = NEAR * RB_DEV
    width = 2 * half + 1
    rows = jnp.arange(NBR, dtype=jnp.int32)[:, None]
    offsets = jnp.arange(-half, half + 1, dtype=jnp.int32)[None, :]
    candidate = rows + offsets
    scores = jax.random.randint(key, (NBR, width), 0, 1 << 20) * width + jnp.arange(width, dtype=jnp.int32)[None, :]
    scores = jnp.where((candidate < 0) | (candidate >= NBR), -1, scores)
    scores = jnp.where(offsets == 0, (1 << 20) * width + width, scores)
    values, picks = lax.top_k(scores, NNZ)
    chosen = jnp.take_along_axis(candidate, picks, axis=1)
    return jnp.sort(chosen, axis=1).astype(jnp.int32)


def block_levels(own_key, dims, split, low, largest):
    loudness, own = 1.0, jax.random.fold_in(own_key, 6)
    for position, shards_of in split:
        heights = jnp.exp(jax.random.uniform(jax.random.fold_in(own, position), (shards_of,), jnp.float32, low / len(split), largest / len(split)))
        loudness = loudness * jnp.repeat(heights, dims[position] // shards_of).reshape([-1 if axis == position else 1 for axis in range(len(dims))])
    return loudness


def normal_values(key, shape, spread, reach, split=(), kind=jnp.bfloat16):
    level = block_levels(key, shape, split, -0.22, 0.18) if split else 1.0
    entries = jax.random.normal(key, shape, jnp.float32) * spread * level
    return jnp.minimum(jnp.maximum(entries, -reach), reach).astype(kind)


def setup_inputs(seed: int = 0) -> dict:
    streams_of = jax.random.split(jax.random.key(seed), 3)
    density_blocks = normal_values(streams_of[0], (NBR, NNZ, BS, BS), (NNZ * BS) ** -0.5, 0.15625, ((0, 128),), jnp.float32)
    block_cols = draw_block_cols(jax.random.fold_in(streams_of[2], 71), 0)
    return {"density_blocks": density_blocks, "block_cols": block_cols}


def reference(density_blocks, block_cols):
    highest = lax.Precision.HIGHEST

    def one_row(index):
        own_cols = block_cols[index]
        near_blocks = density_blocks[own_cols]
        near_cols = block_cols[own_cols]
        match = (near_cols[:, :, None] == own_cols[None, None, :]).astype(jnp.float32)
        picked = jnp.einsum("kab,kaxy->kbxy", match, near_blocks, precision=highest)
        square = jnp.einsum("kxz,kbzy->bxy", density_blocks[index], picked, precision=highest)
        cube = jnp.einsum("kxz,kbzy->bxy", square, picked, precision=highest)
        return 3.0 * square - 2.0 * cube

    return lax.map(one_row, jnp.arange(NBR, dtype=jnp.int32))
```

```python
import functools

import jax
import jax.numpy as jnp
from jax import lax
from jax.experimental import pallas as pl
from jax.experimental.pallas import tpu as pltpu
from jax.sharding import PartitionSpec as P

MESH = pl.DeviceIdType.MESH
BS = 128
NNZ = 12
NEAR = 3
RB = 4
OWN = RB * NNZ
SLOTS = 2 * NEAR + 1
ZERO = SLOTS * OWN
STEPS = 8
CH = OWN // STEPS
QB = 4
TROWS = SLOTS * 8


def split(x):
    high = x.astype(jnp.bfloat16)
    return high, (x - high.astype(jnp.float32)).astype(jnp.bfloat16)


def dot3(lhs_hi, lhs_lo, rhs_hi, rhs_lo):
    dot = functools.partial(jnp.dot, preferred_element_type=jnp.float32)
    return dot(lhs_hi, rhs_hi) + dot(lhs_lo, rhs_hi) + dot(lhs_hi, rhs_lo)


def kernel(
    n,
    x_ref,
    colv_ref,
    cols,
    out_ref,
    win,
    hi,
    lo,
    sq,
    sq_hi,
    sq_lo,
    colbuf,
    wcols,
    tab_v,
    tab,
    s_cols,
    r_cols,
    s_own,
    r_own,
    s_fwd,
    r_fwd,
    s_part,
    r_part,
    s_local,
):
    d = lax.axis_index("grid")
    p = lax.rem(d, 2)
    right, left = lax.rem(d + 2, n), lax.rem(d + n - 2, n)
    partner = d + 1 - 2 * p
    far_dev = lax.rem(d + n - 1 + 2 * p, n)
    far = 6 * p
    base = RB * (d - NEAR)
    offsets = (-3, -2, -1, 1, 2, 3)

    barrier = pltpu.get_barrier_semaphore()
    for off in offsets:
        pl.semaphore_signal(
            barrier, inc=1, device_id=(lax.rem(d + n + off, n),), device_id_type=MESH
        )
    load = pltpu.make_async_copy(x_ref, win.at[NEAR], s_local.at[0])
    load.start()
    colbuf[...] = jnp.full((8, 128), -1, jnp.int32)
    colbuf[0:RB, 0:NNZ] = colv_ref[...]
    wcols[NEAR] = colbuf[...]
    pl.semaphore_wait(barrier, len(offsets))

    def remote(src, dst, send, recv, dev):
        return pltpu.make_async_remote_copy(
            src_ref=src,
            dst_ref=dst,
            send_sem=send,
            recv_sem=recv,
            device_id=(dev,),
            device_id_type=MESH,
        )

    def col_copy(m):
        off = offsets[m]
        return remote(
            colbuf,
            wcols.at[NEAR - off],
            s_cols.at[m],
            r_cols.at[m],
            lax.rem(d + n + off, n),
        )

    for m in range(len(offsets)):
        col_copy(m).start()

    def at_right(u):
        return (RB - 1 - u // 2) * NNZ + lax.rem(u, 2) * CH

    def at_left(u):
        return (u // 2) * NNZ + lax.rem(u, 2) * CH

    def own_right(u):
        pos = at_right(u)
        return remote(
            x_ref.at[pl.ds(pos, CH)],
            win.at[1, pl.ds(pos, CH)],
            s_own.at[0, u],
            r_own.at[0, u],
            right,
        )

    def own_left(u):
        pos = at_left(u)
        return remote(
            x_ref.at[pl.ds(pos, CH)],
            win.at[5, pl.ds(pos, CH)],
            s_own.at[1, u],
            r_own.at[1, u],
            left,
        )

    def part_copy():
        return remote(
            x_ref, win.at[2 + 2 * p], s_part.at[0], r_part.at[0], partner
        )

    def start_own(u, carry):
        own_right(u).start()
        own_left(u).start()
        return carry

    lax.fori_loop(0, STEPS, start_own, 0)
    part_copy().start()

    def convert(slot, pos, count):
        h, l = split(win[slot, pl.ds(pos, count)])
        hi[pl.ds(slot * OWN + pos, count)] = h
        lo[pl.ds(slot * OWN + pos, count)] = l

    def convert_all(slot):
        def step(u, carry):
            convert(slot, u * CH, CH)
            return carry

        lax.fori_loop(0, STEPS, step, 0)

    hi[ZERO] = jnp.zeros((BS, BS), jnp.bfloat16)
    lo[ZERO] = jnp.zeros((BS, BS), jnp.bfloat16)
    load.wait()
    convert_all(NEAR)

    for m in range(len(offsets)):
        col_copy(m).wait()
    row_in_tile = lax.broadcasted_iota(jnp.int32, (8, 128), 0)
    own_tile = wcols[NEAR]
    for i in range(RB):
        own_cols = jnp.broadcast_to(own_tile[i : i + 1, :], (8, 128))

        def slot_table(s, carry):
            tile = wcols[s]
            found = jnp.full((8, 128), ZERO, jnp.int32)
            first = (s * RB + row_in_tile) * NNZ
            for t in range(NNZ):
                col = jnp.broadcast_to(tile[:, t : t + 1], (8, 128))
                found = jnp.where(col == own_cols, first + t, found)
            tab_v[pl.ds(pl.multiple_of(i * TROWS + s * 8, 8), 8), :] = jnp.where(
                row_in_tile < RB, found, ZERO
            )
            return carry

        lax.fori_loop(0, SLOTS, slot_table, 0)
    lane = lax.broadcasted_iota(jnp.int32, (8, 128), 1)
    coef = jnp.full((8, 128), ZERO, jnp.int32)
    for a in range(NNZ):
        col = jnp.broadcast_to(own_tile[:, a : a + 1], (8, 128))
        coef = jnp.where(col == lane + base, NEAR * OWN + row_in_tile * NNZ + a, coef)
    tab_v[RB * TROWS : RB * TROWS + 8, :] = jnp.where(row_in_tile < RB, coef, ZERO)
    to_smem = pltpu.make_async_copy(tab_v, tab, s_local.at[1])
    to_smem.start()
    to_smem.wait()

    def fwd_from_left(u):
        pos = at_right(u)
        return remote(
            win.at[1, pl.ds(pos, CH)],
            win.at[2 * p, pl.ds(pos, CH)],
            s_fwd.at[0, u],
            r_fwd.at[0, u],
            partner,
        )

    def fwd_from_right(u):
        pos = at_left(u)
        return remote(
            win.at[5, pl.ds(pos, CH)],
            win.at[4 + 2 * p, pl.ds(pos, CH)],
            s_fwd.at[1, u],
            r_fwd.at[1, u],
            partner,
        )

    def fwd_far(u):
        pos = at_right(u) * p + at_left(u) * (1 - p)
        return remote(
            win.at[5 - 4 * p, pl.ds(pos, CH)],
            win.at[6 - 6 * p, pl.ds(pos, CH)],
            s_fwd.at[2, u],
            r_fwd.at[2, u],
            far_dev,
        )

    def take_partner(u):
        fwd_from_left(u).wait_recv()
        convert(2 - 2 * p, at_right(u), CH)
        fwd_from_right(u).wait_recv()
        convert(6 - 2 * p, at_left(u), CH)

    part_copy().wait_recv()
    convert_all(4 - 2 * p)

    def near_step(u, carry):
        own_right(u).wait_recv()
        own_left(u).wait_recv()
        fwd_from_left(u).start()
        fwd_from_right(u).start()
        fwd_far(u).start()
        convert(1, at_right(u), CH)
        convert(5, at_left(u), CH)
        take_partner(u)
        return carry

    lax.fori_loop(0, STEPS, near_step, 0)

    def tile(ref, index, count_a):
        return jnp.concatenate(
            [
                jnp.concatenate([ref[index[a][b]] for b in range(QB)], axis=1)
                for a in range(count_a)
            ],
            axis=0,
        )

    def window_rows(i):
        rows = []
        for a in range(NNZ):
            r = jnp.clip(cols[i, a] - base, 0, SLOTS * RB - 1)
            rows.append((r, i * TROWS + r + lax.shift_left(lax.shift_right_logical(r, 2), 2)))
        return rows

    def part(q):
        return pl.ds(pl.multiple_of(q * QB * BS, QB * BS), QB * BS)

    def near_square(i, carry):
        rows = window_rows(i)

        def columns(q, carry):
            index = []
            for r, row in rows:
                in_far = jnp.logical_and(r >= far * RB, r < far * RB + RB)
                index.append(
                    [jnp.where(in_far, ZERO, tab[row, q * QB + b]) for b in range(QB)]
                )
            own = NEAR * OWN + i * NNZ
            lhs_hi = jnp.concatenate([hi[own + a] for a in range(NNZ)], axis=1)
            lhs_lo = jnp.concatenate([lo[own + a] for a in range(NNZ)], axis=1)
            sq[i, :, part(q)] = dot3(
                lhs_hi, lhs_lo, tile(hi, index, NNZ), tile(lo, index, NNZ)
            )
            return carry

        lax.fori_loop(0, NNZ // QB, columns, 0)
        return carry

    lax.fori_loop(0, RB, near_square, 0)

    def far_square(i, j):
        at = tab[RB * TROWS + i, far * RB + j]
        lhs_hi, lhs_lo = hi[at], lo[at]

        def columns(q, carry):
            index = [[tab[i * TROWS + far * 8 + j, q * QB + b] for b in range(QB)]]
            sq[i, :, part(q)] += dot3(lhs_hi, lhs_lo, tile(hi, index, 1), tile(lo, index, 1))
            return carry

        lax.fori_loop(0, NNZ // QB, columns, 0)

    def out_copy(i):
        rows = pl.ds(i * NNZ, NNZ)
        return pltpu.make_async_copy(win.at[NEAR, rows], out_ref.at[rows], s_local.at[2 + i])

    def cube(i):
        h, l = split(sq[i])
        sq_hi[...] = h
        sq_lo[...] = l
        rows = window_rows(i)

        def columns(q, carry):
            index = [[tab[row, q * QB + b] for b in range(QB)] for _, row in rows]
            third = dot3(sq_hi[...], sq_lo[...], tile(hi, index, NNZ), tile(lo, index, NNZ))
            res = 3.0 * sq[i, :, part(q)] - 2.0 * third
            for b in range(QB):
                win[NEAR, i * NNZ + q * QB + b] = res[:, b * BS : (b + 1) * BS]
            return carry

        lax.fori_loop(0, NNZ // QB, columns, 0)
        out_copy(i).start()

    def far_step(t, carry):
        j = (RB - 1 - t) * (1 - p) + t * p
        for half in range(2):
            u = 2 * t + half
            pos = at_right(u) * (1 - p) + at_left(u) * p
            fwd_far(u).wait_recv()
            convert(far, pos, CH)

        def row(m, carry):
            far_square(m * (1 - p) + (RB - 1 - m) * p, j)
            return carry

        lax.fori_loop(0, RB - t, row, 0)
        last = RB - 1 - t
        cube(last * (1 - p) + (RB - 1 - last) * p)
        return carry

    lax.fori_loop(0, RB, far_step, 0)

    def finish(u, carry):
        own_right(u).wait_send()
        own_left(u).wait_send()
        fwd_from_left(u).wait_send()
        fwd_from_right(u).wait_send()
        fwd_far(u).wait_send()
        return carry

    lax.fori_loop(0, STEPS, finish, 0)
    part_copy().wait_send()
    for i in range(RB):
        out_copy(i).wait()


def body(density_blocks, block_cols, n):
    blocks = density_blocks.reshape(OWN, BS, BS)
    dma = pltpu.SemaphoreType.DMA
    out = pl.pallas_call(
        functools.partial(kernel, n),
        out_shape=jax.ShapeDtypeStruct((OWN, BS, BS), jnp.float32),
        in_specs=[
            pl.BlockSpec(memory_space=pl.ANY),
            pl.BlockSpec(memory_space=pltpu.VMEM),
            pl.BlockSpec(memory_space=pltpu.SMEM),
        ],
        out_specs=pl.BlockSpec(memory_space=pl.ANY),
        scratch_shapes=[
            pltpu.VMEM((SLOTS, OWN, BS, BS), jnp.float32),
            pltpu.VMEM((ZERO + 1, BS, BS), jnp.bfloat16),
            pltpu.VMEM((ZERO + 1, BS, BS), jnp.bfloat16),
            pltpu.VMEM((RB, BS, NNZ * BS), jnp.float32),
            pltpu.VMEM((BS, NNZ * BS), jnp.bfloat16),
            pltpu.VMEM((BS, NNZ * BS), jnp.bfloat16),
            pltpu.VMEM((8, 128), jnp.int32),
            pltpu.VMEM((SLOTS, 8, 128), jnp.int32),
            pltpu.VMEM((RB * TROWS + 8, 128), jnp.int32),
            pltpu.SMEM((RB * TROWS + 8, 128), jnp.int32),
            dma((6,)),
            dma((6,)),
            dma((2, STEPS)),
            dma((2, STEPS)),
            dma((3, STEPS)),
            dma((3, STEPS)),
            dma((1,)),
            dma((1,)),
            dma((2 + RB,)),
        ],
        compiler_params=pltpu.CompilerParams(
            collective_id=0, has_side_effects=True, vmem_limit_bytes=58 << 20
        ),
        name="mcweeny",
    )(blocks, block_cols, block_cols)
    return out.reshape(RB, NNZ, BS, BS)


def solution(mesh):
    placed = (P("grid", None, None, None), P("grid", None))
    return jax.shard_map(
        functools.partial(body, n=mesh.shape["grid"]),
        mesh=mesh,
        in_specs=placed,
        out_specs=P("grid", None, None, None),
        check_vma=False,
    )
```

```python
import functools

import jax
import jax.numpy as jnp
from jax import lax
from jax.experimental import pallas as pl
from jax.experimental.pallas import tpu as pltpu
from jax.sharding import PartitionSpec as P

MESH = pl.DeviceIdType.MESH
BS = 128
NNZ = 12
NEAR = 3
RB = 4
OWN = RB * NNZ
SLOTS = 2 * NEAR + 1
ZERO = SLOTS * OWN
STEPS = 8
CH = OWN // STEPS
QB = 4
TROWS = SLOTS * 8


def split(x):
    high = x.astype(jnp.bfloat16)
    return high, (x - high.astype(jnp.float32)).astype(jnp.bfloat16)


def dot3(lhs_hi, lhs_lo, rhs_hi, rhs_lo):
    dot = functools.partial(jnp.dot, preferred_element_type=jnp.float32)
    return dot(lhs_hi, rhs_hi) + dot(lhs_lo, rhs_hi) + dot(lhs_hi, rhs_lo)


def full_kernel(
    n,
    x_ref,
    colv_ref,
    cols,
    out_ref,
    win,
    hi,
    lo,
    sq,
    sq_hi,
    sq_lo,
    colbuf,
    wcols,
    tab_v,
    tab,
    s_cols,
    r_cols,
    s_own,
    r_own,
    s_fwd,
    r_fwd,
    s_part,
    r_part,
    s_local,
):
    d = lax.axis_index("grid")
    p = lax.rem(d, 2)
    right, left = lax.rem(d + 2, n), lax.rem(d + n - 2, n)
    partner = d + 1 - 2 * p
    far_dev = lax.rem(d + n - 1 + 2 * p, n)
    far = 6 * p
    base = RB * (d - NEAR)
    offsets = (-3, -2, -1, 1, 2, 3)

    barrier = pltpu.get_barrier_semaphore()
    for off in offsets:
        pl.semaphore_signal(
            barrier, inc=1, device_id=(lax.rem(d + n + off, n),), device_id_type=MESH
        )
    load = pltpu.make_async_copy(x_ref, win.at[NEAR], s_local.at[0])
    load.start()
    colbuf[...] = jnp.full((8, 128), -1, jnp.int32)
    colbuf[0:RB, 0:NNZ] = colv_ref[...]
    wcols[NEAR] = colbuf[...]
    pl.semaphore_wait(barrier, len(offsets))

    def remote(src, dst, send, recv, dev):
        return pltpu.make_async_remote_copy(
            src_ref=src,
            dst_ref=dst,
            send_sem=send,
            recv_sem=recv,
            device_id=(dev,),
            device_id_type=MESH,
        )

    def col_copy(m):
        off = offsets[m]
        return remote(
            colbuf,
            wcols.at[NEAR - off],
            s_cols.at[m],
            r_cols.at[m],
            lax.rem(d + n + off, n),
        )

    for m in range(len(offsets)):
        col_copy(m).start()

    def at_right(u):
        return (RB - 1 - u // 2) * NNZ + lax.rem(u, 2) * CH

    def at_left(u):
        return (u // 2) * NNZ + lax.rem(u, 2) * CH

    def own_right(u):
        pos = at_right(u)
        return remote(
            x_ref.at[pl.ds(pos, CH)],
            win.at[1, pl.ds(pos, CH)],
            s_own.at[0, u],
            r_own.at[0, u],
            right,
        )

    def own_left(u):
        pos = at_left(u)
        return remote(
            x_ref.at[pl.ds(pos, CH)],
            win.at[5, pl.ds(pos, CH)],
            s_own.at[1, u],
            r_own.at[1, u],
            left,
        )

    def part_copy():
        return remote(
            x_ref, win.at[2 + 2 * p], s_part.at[0], r_part.at[0], partner
        )

    def start_own(u, carry):
        own_right(u).start()
        own_left(u).start()
        return carry

    lax.fori_loop(0, STEPS, start_own, 0)
    part_copy().start()

    def convert(slot, pos, count):
        h, l = split(win[slot, pl.ds(pos, count)])
        hi[pl.ds(slot * OWN + pos, count)] = h
        lo[pl.ds(slot * OWN + pos, count)] = l

    def convert_all(slot):
        def step(u, carry):
            convert(slot, u * CH, CH)
            return carry

        lax.fori_loop(0, STEPS, step, 0)

    hi[ZERO] = jnp.zeros((BS, BS), jnp.bfloat16)
    lo[ZERO] = jnp.zeros((BS, BS), jnp.bfloat16)
    load.wait()
    convert_all(NEAR)

    for m in range(len(offsets)):
        col_copy(m).wait()
    row_in_tile = lax.broadcasted_iota(jnp.int32, (8, 128), 0)
    own_tile = wcols[NEAR]
    for i in range(RB):
        own_cols = jnp.broadcast_to(own_tile[i : i + 1, :], (8, 128))

        def slot_table(s, carry):
            tile = wcols[s]
            found = jnp.full((8, 128), ZERO, jnp.int32)
            first = (s * RB + row_in_tile) * NNZ
            for t in range(NNZ):
                col = jnp.broadcast_to(tile[:, t : t + 1], (8, 128))
                found = jnp.where(col == own_cols, first + t, found)
            tab_v[pl.ds(pl.multiple_of(i * TROWS + s * 8, 8), 8), :] = jnp.where(
                row_in_tile < RB, found, ZERO
            )
            return carry

        lax.fori_loop(0, SLOTS, slot_table, 0)
    lane = lax.broadcasted_iota(jnp.int32, (8, 128), 1)
    coef = jnp.full((8, 128), ZERO, jnp.int32)
    for a in range(NNZ):
        col = jnp.broadcast_to(own_tile[:, a : a + 1], (8, 128))
        coef = jnp.where(col == lane + base, NEAR * OWN + row_in_tile * NNZ + a, coef)
    tab_v[RB * TROWS : RB * TROWS + 8, :] = jnp.where(row_in_tile < RB, coef, ZERO)
    to_smem = pltpu.make_async_copy(tab_v, tab, s_local.at[1])
    to_smem.start()
    to_smem.wait()

    def fwd_from_left(u):
        pos = at_right(u)
        return remote(
            win.at[1, pl.ds(pos, CH)],
            win.at[2 * p, pl.ds(pos, CH)],
            s_fwd.at[0, u],
            r_fwd.at[0, u],
            partner,
        )

    def fwd_from_right(u):
        pos = at_left(u)
        return remote(
            win.at[5, pl.ds(pos, CH)],
            win.at[4 + 2 * p, pl.ds(pos, CH)],
            s_fwd.at[1, u],
            r_fwd.at[1, u],
            partner,
        )

    def fwd_far(u):
        pos = at_right(u) * p + at_left(u) * (1 - p)
        return remote(
            win.at[5 - 4 * p, pl.ds(pos, CH)],
            win.at[6 - 6 * p, pl.ds(pos, CH)],
            s_fwd.at[2, u],
            r_fwd.at[2, u],
            far_dev,
        )

    def take_partner(u):
        fwd_from_left(u).wait_recv()
        convert(2 - 2 * p, at_right(u), CH)
        fwd_from_right(u).wait_recv()
        convert(6 - 2 * p, at_left(u), CH)

    part_copy().wait_recv()
    convert_all(4 - 2 * p)

    def near_step(u, carry):
        own_right(u).wait_recv()
        own_left(u).wait_recv()
        fwd_from_left(u).start()
        fwd_from_right(u).start()
        fwd_far(u).start()
        convert(1, at_right(u), CH)
        convert(5, at_left(u), CH)
        take_partner(u)
        return carry

    lax.fori_loop(0, STEPS, near_step, 0)

    def tile(ref, index, count_a):
        return jnp.concatenate(
            [
                jnp.concatenate([ref[index[a][b]] for b in range(QB)], axis=1)
                for a in range(count_a)
            ],
            axis=0,
        )

    def window_rows(i):
        rows = []
        for a in range(NNZ):
            r = jnp.clip(cols[i, a] - base, 0, SLOTS * RB - 1)
            rows.append((r, i * TROWS + r + lax.shift_left(lax.shift_right_logical(r, 2), 2)))
        return rows

    def part(q):
        return pl.ds(pl.multiple_of(q * QB * BS, QB * BS), QB * BS)

    def near_square(i, carry):
        rows = window_rows(i)

        def columns(q, carry):
            index = []
            for r, row in rows:
                in_far = jnp.logical_and(r >= far * RB, r < far * RB + RB)
                index.append(
                    [jnp.where(in_far, ZERO, tab[row, q * QB + b]) for b in range(QB)]
                )
            own = NEAR * OWN + i * NNZ
            lhs_hi = jnp.concatenate([hi[own + a] for a in range(NNZ)], axis=1)
            lhs_lo = jnp.concatenate([lo[own + a] for a in range(NNZ)], axis=1)
            sq[i, :, part(q)] = dot3(
                lhs_hi, lhs_lo, tile(hi, index, NNZ), tile(lo, index, NNZ)
            )
            return carry

        lax.fori_loop(0, NNZ // QB, columns, 0)
        return carry

    lax.fori_loop(0, RB, near_square, 0)

    def far_square(i, j):
        at = tab[RB * TROWS + i, far * RB + j]
        lhs_hi, lhs_lo = hi[at], lo[at]

        def columns(q, carry):
            index = [[tab[i * TROWS + far * 8 + j, q * QB + b] for b in range(QB)]]
            sq[i, :, part(q)] += dot3(lhs_hi, lhs_lo, tile(hi, index, 1), tile(lo, index, 1))
            return carry

        lax.fori_loop(0, NNZ // QB, columns, 0)

    def out_copy(i):
        rows = pl.ds(i * NNZ, NNZ)
        return pltpu.make_async_copy(win.at[NEAR, rows], out_ref.at[rows], s_local.at[2 + i])

    def cube(i):
        h, l = split(sq[i])
        sq_hi[...] = h
        sq_lo[...] = l
        rows = window_rows(i)

        def columns(q, carry):
            index = [[tab[row, q * QB + b] for b in range(QB)] for _, row in rows]
            third = dot3(sq_hi[...], sq_lo[...], tile(hi, index, NNZ), tile(lo, index, NNZ))
            res = 3.0 * sq[i, :, part(q)] - 2.0 * third
            for b in range(QB):
                win[NEAR, i * NNZ + q * QB + b] = res[:, b * BS : (b + 1) * BS]
            return carry

        lax.fori_loop(0, NNZ // QB, columns, 0)
        out_copy(i).start()

    def far_step(t, carry):
        j = (RB - 1 - t) * (1 - p) + t * p
        for half in range(2):
            u = 2 * t + half
            pos = at_right(u) * (1 - p) + at_left(u) * p
            fwd_far(u).wait_recv()
            convert(far, pos, CH)

        def row(m, carry):
            far_square(m * (1 - p) + (RB - 1 - m) * p, j)
            return carry

        lax.fori_loop(0, RB - t, row, 0)
        last = RB - 1 - t
        cube(last * (1 - p) + (RB - 1 - last) * p)
        return carry

    lax.fori_loop(0, RB, far_step, 0)

    def finish(u, carry):
        own_right(u).wait_send()
        own_left(u).wait_send()
        fwd_from_left(u).wait_send()
        fwd_from_right(u).wait_send()
        fwd_far(u).wait_send()
        return carry

    lax.fori_loop(0, STEPS, finish, 0)
    part_copy().wait_send()
    for i in range(RB):
        out_copy(i).wait()


X = 24
CAP = 68
PCH = 4
PSTEPS = CAP // PCH
ASTEPS = OWN // PCH
PART0, RAW_A0, RAW_B0, POOL_A0, POOL_B0 = 48, 96, 144, 192, 192 + CAP
NONE = POOL_B0 + OWN
AHEAD = 3
ROUNDS = 7
PAD = -100000


def fast_kernel(
    n,
    x_ref,
    colv_ref,
    cols,
    out_ref,
    flag_ref,
    own,
    part,
    raw_a,
    raw_b,
    pool_a,
    pool_b,
    pool_out,
    hi,
    lo,
    sq,
    sq_hi,
    sq_lo,
    colbuf,
    wcols,
    mapbuf,
    maps,
    inv_v,
    inv,
    tab_v,
    tab,
    idx,
    fbuf,
    fin,
    s_cols,
    r_cols,
    s_map,
    r_map,
    s_raw,
    r_raw,
    s_pool,
    r_pool,
    s_fraw,
    r_fraw,
    s_fpool,
    r_fpool,
    s_part,
    r_part,
    s_flag,
    r_flag,
    s_local,
):
    f32, i32 = jnp.float32, jnp.int32
    d = lax.axis_index("grid")
    p = lax.rem(d, 2)
    s = 2 * p - 1
    base = RB * (d - NEAR)
    offsets = (-3, -2, -1, 1, 2, 3)

    def at(off):
        return lax.rem(d + n + off, n)

    def flip(r):
        bit = 1 << r if isinstance(r, int) else 16 + (r - 4) * 16 + jnp.maximum(r - 5, 0) * 16
        return d + bit - 2 * bit * lax.rem(d // bit, 2)

    ahead, ahead2, partner = at(s), at(2 * s), at(-s)

    barrier = pltpu.get_barrier_semaphore()
    greeted = [at(off) for off in offsets] + [flip(r) for r in range(2, ROUNDS)]
    for dev in greeted:
        pl.semaphore_signal(barrier, inc=1, device_id=(dev,), device_id_type=MESH)
    load = pltpu.make_async_copy(x_ref, own, s_local.at[0])
    load.start()
    colbuf[...] = jnp.full((8, 128), PAD, i32)
    colbuf[0:RB, 0:NNZ] = colv_ref[...]
    wcols[NEAR] = colbuf[...]
    pl.semaphore_wait(barrier, len(greeted))

    def remote(src, dst, send, recv, dev):
        return pltpu.make_async_remote_copy(
            src_ref=src,
            dst_ref=dst,
            send_sem=send,
            recv_sem=recv,
            device_id=(dev,),
            device_id_type=MESH,
        )

    def col_copy(m):
        off = offsets[m]
        return remote(colbuf, wcols.at[NEAR - off], s_cols.at[m], r_cols.at[m], at(off))

    def part_copy():
        return remote(x_ref, part, s_part.at[0], r_part.at[0], partner)

    def raw_copy(u):
        rows = pl.ds(u * CH, CH)
        return remote(x_ref.at[rows], raw_a.at[rows], s_raw.at[u], r_raw.at[u], ahead)

    def raw_fwd(u):
        rows = pl.ds(u * CH, CH)
        return remote(raw_a.at[rows], raw_b.at[rows], s_fraw.at[u], r_fraw.at[u], partner)

    def pool_copy(u):
        rows = pl.ds(u * PCH, PCH)
        return remote(pool_out.at[rows], pool_a.at[rows], s_pool.at[u], r_pool.at[u], ahead)

    def pool_fwd(u):
        rows = pl.ds(u * PCH, PCH)
        return remote(pool_a.at[rows], pool_b.at[rows], s_fpool.at[u], r_fpool.at[u], partner)

    def map_copy(m):
        return remote(
            mapbuf, maps.at[m], s_map.at[m], r_map.at[m], ahead if m == 0 else ahead2
        )

    def flag_copy(r):
        return remote(fbuf.at[r], fin.at[r], s_flag.at[r], r_flag.at[r], flip(r))

    def finish_round(r):
        flag_copy(r).wait_recv()
        fbuf[r + 1] = jnp.maximum(fbuf[r], fin[r])

    for m in range(len(offsets)):
        col_copy(m).start()

    def start_raw(u, carry):
        raw_copy(u).start()
        return carry

    lax.fori_loop(0, AHEAD, start_raw, 0)
    part_copy().start()

    def convert(ref, first, pos, count):
        h, l = split(ref[pl.ds(pos, count)])
        hi[pl.ds(first + pos, count)] = h
        lo[pl.ds(first + pos, count)] = l

    def convert_all(ref, first):
        def step(u, carry):
            convert(ref, first, u * CH, CH)
            return carry

        lax.fori_loop(0, STEPS, step, 0)

    hi[NONE] = jnp.zeros((BS, BS), jnp.bfloat16)
    lo[NONE] = jnp.zeros((BS, BS), jnp.bfloat16)

    for m in range(len(offsets)):
        col_copy(m).wait_recv()
    sub = lax.broadcasted_iota(i32, (8, 128), 0)
    lane = lax.broadcasted_iota(i32, (8, 128), 1)
    lane_col = lane + (RB * d - 64)

    def spread(tile, value):
        where = jnp.zeros((8, 128), f32)
        what = jnp.zeros((8, 128), i32)
        for t in range(NNZ):
            hit = jnp.broadcast_to(tile[:, t : t + 1], (8, 128)) == lane_col
            where = jnp.where(hit, 1.0, where)
            if value is not None:
                what = jnp.where(hit, value + t, what)
        return where, what

    next1, _ = spread(wcols[NEAR + s], None)
    next2, _ = spread(wcols[NEAR + 2 * s], None)

    def needed(readers, back):
        need = jnp.zeros((8, 128), f32)
        for j in range(RB):
            here = lane == 64 - RB * back * s + j
            row = jnp.zeros((1, 128), f32)
            for reader in readers:
                reads = jnp.max(jnp.where(here, reader, 0.0), axis=1, keepdims=True)
                row = jnp.maximum(row, jnp.max(reader * reads, axis=0, keepdims=True))
            need = jnp.where(sub == j, jnp.broadcast_to(row, (8, 128)), need)
        return need

    has_1, src_1 = spread(wcols[NEAR - s], sub * NNZ)
    has_2, src_2 = spread(wcols[NEAR - 2 * s], sub * NNZ + OWN)
    chosen = jnp.concatenate(
        [has_1 * needed([next1, next2], 1), has_2 * needed([next1], 2)], axis=0
    )
    square_row = lax.broadcasted_iota(i32, (128, 128), 0)
    square_lane = lax.broadcasted_iota(i32, (128, 128), 1)
    before = jnp.where(square_row < square_lane, 1.0, 0.0).astype(jnp.bfloat16)
    rank = jnp.dot(chosen.astype(jnp.bfloat16), before, preferred_element_type=f32)
    totals = jnp.sum(chosen, axis=1, keepdims=True)
    sub16 = lax.broadcasted_iota(i32, (16, 128), 0)
    count_1 = jnp.zeros((1, 1), f32)
    count_2 = jnp.zeros((1, 1), f32)
    for j in range(RB):
        count_1 = count_1 + totals[j : j + 1, :]
        count_2 = count_2 + totals[8 + j : 9 + j, :]
    start_2 = jnp.maximum(count_1, float(X))
    for r in range(RB):
        rank = rank + jnp.where(
            jnp.logical_and(sub16 > r, sub16 < 8),
            jnp.broadcast_to(totals[r : r + 1, :], (16, 128)),
            0.0,
        )
        rank = rank + jnp.where(
            sub16 > 8 + r, jnp.broadcast_to(totals[8 + r : 9 + r, :], (16, 128)), 0.0
        )
    rank = rank + jnp.where(sub16 >= 8, jnp.broadcast_to(start_2, (16, 128)), 0.0)
    taken = jnp.logical_and(chosen > 0.5, rank < CAP - 0.5)
    slot = jnp.where(taken, rank, -1.0)
    slot_int = slot.astype(i32)
    mapbuf[...] = slot_int
    for m in range(2):
        map_copy(m).start()
    over = jnp.where(start_2 + count_2 > CAP + 0.5, 1.0, 0.0)
    fbuf[0] = jnp.broadcast_to(over, (8, 128))

    for tile in range(-(-CAP // 8)):
        found = jnp.zeros((8, 128), i32)
        for r in range(RB):
            hit = jnp.broadcast_to(slot_int[r : r + 1, :], (8, 128)) == sub + 8 * tile
            found = jnp.where(hit, jnp.broadcast_to(src_1[r : r + 1, :], (8, 128)), found)
            if tile * 8 >= X:
                hit = jnp.broadcast_to(slot_int[8 + r : 9 + r, :], (8, 128)) == sub + 8 * tile
                found = jnp.where(hit, jnp.broadcast_to(src_2[r : r + 1, :], (8, 128)), found)
        source = jnp.sum(found.astype(f32), axis=1, keepdims=True).astype(i32)
        inv_v[tile * 8 : tile * 8 + 8, :] = jnp.broadcast_to(source, (8, 128))
    to_inv = pltpu.make_async_copy(inv_v, inv, s_local.at[1])
    to_inv.start()
    to_inv.wait()

    part_copy().wait_recv()

    def pack_first(u, carry):
        for b in range(PCH):
            pool_out[u * PCH + b] = part[jnp.clip(inv[u * PCH + b, 0], 0, OWN - 1)]
        return carry

    lax.fori_loop(0, X // PCH, pack_first, 0)
    load.wait()
    convert_all(own, 0)
    convert_all(part, PART0)

    def lane_base(o):
        back = jnp.where(o >= 2, s, jnp.where(o <= -3, -2 * s, 0))
        return RB * (d + back) - 64

    def resolve(m, carry):
        i = m // NNZ
        r = jnp.clip(cols[i, lax.rem(m, NNZ)] - base, 0, SLOTS * RB - 1)
        w = lax.shift_right_logical(r, 2)
        row = w * 8 + lax.bitwise_and(r, 3)
        first = lane_base(s * (w - NEAR))
        for b in range(NNZ):
            found = tab[row, jnp.clip(cols[i, b] - first, 0, 127)]
            idx[m * NNZ + b] = jnp.clip(found, 0, NONE)
        return carry

    def take_raw_b(u):
        raw_fwd(u).wait_recv()
        convert(raw_b, RAW_B0, u * CH, CH)

    def build_table():
        for m in range(2):
            map_copy(m).wait_recv()

        def put(o, tile):
            at_row = pl.multiple_of((NEAR + s * o) * 8, 8)
            tab_v[pl.ds(at_row, 8), :] = jnp.where(sub < RB, jnp.clip(tile, 0, NONE), NONE)

        for o, first in ((0, 0), (-1, PART0), (1, RAW_A0), (-2, RAW_B0)):
            has, where = spread(wcols[NEAR + s * o], sub * NNZ + first)
            put(o, jnp.where(has > 0.5, where, NONE))
        for o, m, half, first in ((2, 0, 0, POOL_A0), (3, 0, 8, POOL_A0), (-3, 1, 0, POOL_B0)):
            got = maps[m, half : half + 8, :]
            put(o, jnp.where(got >= 0, got + first, NONE))
        to_tab = pltpu.make_async_copy(tab_v, tab, s_local.at[1])
        to_tab.start()
        to_tab.wait()

    for u in range(STEPS):
        raw_copy(u).wait_recv()
        raw_fwd(u).start()
        if u % 2 == 0:
            if u > 0:
                finish_round(u // 2 - 1)
            flag_copy(u // 2).start()
        if u + AHEAD < STEPS:
            raw_copy(u + AHEAD).start()
        else:
            pool_copy(u + AHEAD - STEPS).start()
        convert(raw_a, RAW_A0, u * CH, CH)
        if u > 0:
            take_raw_b(u - 1)
        if u == 3:
            build_table()
    take_raw_b(STEPS - 1)

    def pack_rest(u, carry):
        for b in range(PCH):
            source = inv[u * PCH + b, 0]
            pool_out[u * PCH + b] = jnp.where(
                source < OWN,
                part[jnp.clip(source, 0, OWN - 1)],
                raw_b[jnp.clip(source - OWN, 0, OWN - 1)],
            )
        pool_copy(u).start()
        return carry

    def take_pool_b(u):
        pool_fwd(u).wait_recv()
        convert(pool_b, POOL_B0, u * PCH, PCH)

    def pool_step(u, carry):
        pool_copy(u).wait_recv()
        pool_fwd(u).start()

        @pl.when(u + AHEAD < X // PCH)
        def _():
            pool_copy(u + AHEAD).start()

        @pl.when(u + AHEAD >= X // PCH)
        def _():
            pack_rest(u + AHEAD, 0)

        convert(pool_a, POOL_A0, u * PCH, PCH)

        @pl.when(u > 0)
        def _():
            take_pool_b(u - 1)

        lax.fori_loop(u * RB, (u + 1) * RB, resolve, 0)
        return carry

    finish_round(STEPS // 2 - 1)
    lax.fori_loop(0, ASTEPS, pool_step, 0)
    lax.fori_loop(ASTEPS + AHEAD, PSTEPS, pack_rest, 0)
    take_pool_b(ASTEPS - 1)

    def tile(ref, index, count_a):
        return jnp.concatenate(
            [
                jnp.concatenate([ref[index[a][b]] for b in range(QB)], axis=1)
                for a in range(count_a)
            ],
            axis=0,
        )

    def block_at(i, a, b):
        return jnp.clip(idx[(i * NNZ + a) * NNZ + b], 0, NONE)

    def part_of(q):
        return pl.ds(q * QB * BS, QB * BS)

    def near_square(i, carry):
        keep = []
        for a in range(NNZ):
            r = jnp.clip(cols[i, a] - base, 0, SLOTS * RB - 1)
            keep.append(s * (lax.shift_right_logical(r, 2) - NEAR) < 3)
        lhs_hi = jnp.concatenate([hi[i * NNZ + a] for a in range(NNZ)], axis=1)
        lhs_lo = jnp.concatenate([lo[i * NNZ + a] for a in range(NNZ)], axis=1)
        for q in range(NNZ // QB):
            index = [
                [
                    jnp.where(keep[a], block_at(i, a, q * QB + b), NONE)
                    for b in range(QB)
                ]
                for a in range(NNZ)
            ]
            sq[i, :, part_of(q)] = dot3(
                lhs_hi, lhs_lo, tile(hi, index, NNZ), tile(lo, index, NNZ)
            )
        return carry

    lax.fori_loop(0, RB, near_square, 0)

    def last_pool(u, carry):
        pool_copy(u).wait_recv()
        convert(pool_a, POOL_A0, u * PCH, PCH)
        return carry

    lax.fori_loop(ASTEPS, PSTEPS, last_pool, 0)

    far_base = lane_base(3)

    def out_copy(i):
        rows = pl.ds(i * NNZ, NNZ)
        return pltpu.make_async_copy(own.at[rows], out_ref.at[rows], s_local.at[2 + i])

    def finish_row(i, carry):
        r = STEPS // 2 + i

        @pl.when(i < RB - 1)
        def _():
            flag_copy(r).start()

        coef = [
            jnp.clip(tab[NEAR * 8 + i, 64 + 3 * RB * s + j], 0, NONE) for j in range(RB)
        ]
        lhs_hi = jnp.concatenate([hi[c] for c in coef], axis=1)
        lhs_lo = jnp.concatenate([lo[c] for c in coef], axis=1)
        lanes = [jnp.clip(cols[i, b] - far_base, 0, 127) for b in range(NNZ)]
        for q in range(NNZ // QB):
            index = [
                [
                    jnp.clip(tab[(NEAR + 3 * s) * 8 + j, lanes[q * QB + b]], 0, NONE)
                    for b in range(QB)
                ]
                for j in range(RB)
            ]
            sq[i, :, part_of(q)] += dot3(
                lhs_hi, lhs_lo, tile(hi, index, RB), tile(lo, index, RB)
            )
        h, l = split(sq[i])
        sq_hi[...] = h
        sq_lo[...] = l
        for q in range(NNZ // QB):
            index = [
                [block_at(i, a, q * QB + b) for b in range(QB)]
                for a in range(NNZ)
            ]
            third = dot3(sq_hi[...], sq_lo[...], tile(hi, index, NNZ), tile(lo, index, NNZ))
            res = 3.0 * sq[i, :, part_of(q)] - 2.0 * third
            for b in range(QB):
                own[i * NNZ + q * QB + b] = res[:, b * BS : (b + 1) * BS]
        out_copy(i).start()

        @pl.when(i < RB - 1)
        def _():
            finish_round(r)

        return carry

    lax.fori_loop(0, RB, finish_row, 0)
    flag_ref[...] = fbuf[ROUNDS]

    def done_raw(u, carry):
        raw_copy(u).wait_send()
        raw_fwd(u).wait_send()
        return carry

    def done_pool(u, carry):
        pool_copy(u).wait_send()
        return carry

    def done_fwd(u, carry):
        pool_fwd(u).wait_send()
        return carry

    lax.fori_loop(0, STEPS, done_raw, 0)
    lax.fori_loop(0, PSTEPS, done_pool, 0)
    lax.fori_loop(0, ASTEPS, done_fwd, 0)
    part_copy().wait_send()
    for m in range(len(offsets)):
        col_copy(m).wait_send()
    for m in range(2):
        map_copy(m).wait_send()
    for r in range(ROUNDS):
        flag_copy(r).wait_send()
    for i in range(RB):
        out_copy(i).wait()


def call_full(blocks, block_cols, n):
    dma = pltpu.SemaphoreType.DMA
    return pl.pallas_call(
        functools.partial(full_kernel, n),
        out_shape=jax.ShapeDtypeStruct((OWN, BS, BS), jnp.float32),
        in_specs=[
            pl.BlockSpec(memory_space=pl.ANY),
            pl.BlockSpec(memory_space=pltpu.VMEM),
            pl.BlockSpec(memory_space=pltpu.SMEM),
        ],
        out_specs=pl.BlockSpec(memory_space=pl.ANY),
        scratch_shapes=[
            pltpu.VMEM((SLOTS, OWN, BS, BS), jnp.float32),
            pltpu.VMEM((ZERO + 1, BS, BS), jnp.bfloat16),
            pltpu.VMEM((ZERO + 1, BS, BS), jnp.bfloat16),
            pltpu.VMEM((RB, BS, NNZ * BS), jnp.float32),
            pltpu.VMEM((BS, NNZ * BS), jnp.bfloat16),
            pltpu.VMEM((BS, NNZ * BS), jnp.bfloat16),
            pltpu.VMEM((8, 128), jnp.int32),
            pltpu.VMEM((SLOTS, 8, 128), jnp.int32),
            pltpu.VMEM((RB * TROWS + 8, 128), jnp.int32),
            pltpu.SMEM((RB * TROWS + 8, 128), jnp.int32),
            dma((6,)),
            dma((6,)),
            dma((2, STEPS)),
            dma((2, STEPS)),
            dma((3, STEPS)),
            dma((3, STEPS)),
            dma((1,)),
            dma((1,)),
            dma((2 + RB,)),
        ],
        compiler_params=pltpu.CompilerParams(
            collective_id=1, has_side_effects=True, vmem_limit_bytes=58 << 20
        ),
        name="mcweeny_full",
    )(blocks, block_cols, block_cols)


def call_fast(blocks, block_cols, n):
    dma = pltpu.SemaphoreType.DMA
    buffer = lambda count: pltpu.VMEM((count, BS, BS), jnp.float32)
    half = pltpu.VMEM((NONE + 1, BS, BS), jnp.bfloat16)
    rows = -(-CAP // 8) * 8
    return pl.pallas_call(
        functools.partial(fast_kernel, n),
        out_shape=[
            jax.ShapeDtypeStruct((OWN, BS, BS), jnp.float32),
            jax.ShapeDtypeStruct((8, 128), jnp.float32),
        ],
        in_specs=[
            pl.BlockSpec(memory_space=pl.ANY),
            pl.BlockSpec(memory_space=pltpu.VMEM),
            pl.BlockSpec(memory_space=pltpu.SMEM),
        ],
        out_specs=[
            pl.BlockSpec(memory_space=pl.ANY),
            pl.BlockSpec(memory_space=pltpu.VMEM),
        ],
        scratch_shapes=[
            buffer(OWN),
            buffer(OWN),
            buffer(OWN),
            buffer(OWN),
            buffer(CAP),
            buffer(OWN),
            buffer(CAP),
            half,
            half,
            pltpu.VMEM((RB, BS, NNZ * BS), jnp.float32),
            pltpu.VMEM((BS, NNZ * BS), jnp.bfloat16),
            pltpu.VMEM((BS, NNZ * BS), jnp.bfloat16),
            pltpu.VMEM((8, 128), jnp.int32),
            pltpu.VMEM((SLOTS, 8, 128), jnp.int32),
            pltpu.VMEM((16, 128), jnp.int32),
            pltpu.VMEM((2, 16, 128), jnp.int32),
            pltpu.VMEM((rows, 128), jnp.int32),
            pltpu.SMEM((rows, 128), jnp.int32),
            pltpu.VMEM((TROWS, 128), jnp.int32),
            pltpu.SMEM((TROWS, 128), jnp.int32),
            pltpu.SMEM((OWN * NNZ,), jnp.int32),
            pltpu.VMEM((ROUNDS + 1, 8, 128), jnp.float32),
            pltpu.VMEM((ROUNDS, 8, 128), jnp.float32),
            dma((6,)),
            dma((6,)),
            dma((2,)),
            dma((2,)),
            dma((STEPS,)),
            dma((STEPS,)),
            dma((PSTEPS,)),
            dma((PSTEPS,)),
            dma((STEPS,)),
            dma((STEPS,)),
            dma((ASTEPS,)),
            dma((ASTEPS,)),
            dma((1,)),
            dma((1,)),
            dma((ROUNDS,)),
            dma((ROUNDS,)),
            dma((2 + RB,)),
        ],
        compiler_params=pltpu.CompilerParams(
            collective_id=0, has_side_effects=True, vmem_limit_bytes=58 << 20
        ),
        name="mcweeny_fast",
    )(blocks, block_cols, block_cols)


def body(density_blocks, block_cols, n):
    blocks = density_blocks.reshape(OWN, BS, BS)
    out, over = call_fast(blocks, block_cols, n)
    out = lax.cond(
        over[0, 0] > 0.5,
        lambda b, c, o: call_full(b, c, n),
        lambda b, c, o: o,
        blocks,
        block_cols,
        out,
    )
    return out.reshape(RB, NNZ, BS, BS)


def solution(mesh):
    placed = (P("grid", None, None, None), P("grid", None))
    return jax.shard_map(
        functools.partial(body, n=mesh.shape["grid"]),
        mesh=mesh,
        in_specs=placed,
        out_specs=P("grid", None, None, None),
        check_vma=False,
    )
```

```python
import functools

import jax
import jax.numpy as jnp
from jax import lax
from jax.experimental import pallas as pl
from jax.experimental.pallas import tpu as pltpu
from jax.sharding import PartitionSpec as P

MESH = pl.DeviceIdType.MESH
BS = 128
NNZ = 12
NEAR = 3
RB = 4
OWN = RB * NNZ
SLOTS = 2 * NEAR + 1
ZERO = SLOTS * OWN
STEPS = 8
CH = OWN // STEPS
QB = 4
TROWS = SLOTS * 8


def split(x):
    high = x.astype(jnp.bfloat16)
    return high, (x - high.astype(jnp.float32)).astype(jnp.bfloat16)


def dot3(lhs_hi, lhs_lo, rhs_hi, rhs_lo):
    dot = functools.partial(jnp.dot, preferred_element_type=jnp.float32)
    return dot(lhs_hi, rhs_hi) + dot(lhs_lo, rhs_hi) + dot(lhs_hi, rhs_lo)


def full_kernel(
    n,
    x_ref,
    colv_ref,
    cols,
    out_ref,
    win,
    hi,
    lo,
    sq,
    sq_hi,
    sq_lo,
    colbuf,
    wcols,
    tab_v,
    tab,
    s_cols,
    r_cols,
    s_own,
    r_own,
    s_fwd,
    r_fwd,
    s_part,
    r_part,
    s_local,
):
    d = lax.axis_index("grid")
    p = lax.rem(d, 2)
    right, left = lax.rem(d + 2, n), lax.rem(d + n - 2, n)
    partner = d + 1 - 2 * p
    far_dev = lax.rem(d + n - 1 + 2 * p, n)
    far = 6 * p
    base = RB * (d - NEAR)
    offsets = (-3, -2, -1, 1, 2, 3)

    barrier = pltpu.get_barrier_semaphore()
    for off in offsets:
        pl.semaphore_signal(
            barrier, inc=1, device_id=(lax.rem(d + n + off, n),), device_id_type=MESH
        )
    load = pltpu.make_async_copy(x_ref, win.at[NEAR], s_local.at[0])
    load.start()
    colbuf[...] = jnp.full((8, 128), -1, jnp.int32)
    colbuf[0:RB, 0:NNZ] = colv_ref[...]
    wcols[NEAR] = colbuf[...]
    pl.semaphore_wait(barrier, len(offsets))

    def remote(src, dst, send, recv, dev):
        return pltpu.make_async_remote_copy(
            src_ref=src,
            dst_ref=dst,
            send_sem=send,
            recv_sem=recv,
            device_id=(dev,),
            device_id_type=MESH,
        )

    def col_copy(m):
        off = offsets[m]
        return remote(
            colbuf,
            wcols.at[NEAR - off],
            s_cols.at[m],
            r_cols.at[m],
            lax.rem(d + n + off, n),
        )

    for m in range(len(offsets)):
        col_copy(m).start()

    def at_right(u):
        return (RB - 1 - u // 2) * NNZ + lax.rem(u, 2) * CH

    def at_left(u):
        return (u // 2) * NNZ + lax.rem(u, 2) * CH

    def own_right(u):
        pos = at_right(u)
        return remote(
            x_ref.at[pl.ds(pos, CH)],
            win.at[1, pl.ds(pos, CH)],
            s_own.at[0, u],
            r_own.at[0, u],
            right,
        )

    def own_left(u):
        pos = at_left(u)
        return remote(
            x_ref.at[pl.ds(pos, CH)],
            win.at[5, pl.ds(pos, CH)],
            s_own.at[1, u],
            r_own.at[1, u],
            left,
        )

    def part_copy():
        return remote(
            x_ref, win.at[2 + 2 * p], s_part.at[0], r_part.at[0], partner
        )

    def start_own(u, carry):
        own_right(u).start()
        own_left(u).start()
        return carry

    lax.fori_loop(0, STEPS, start_own, 0)
    part_copy().start()

    def convert(slot, pos, count):
        h, l = split(win[slot, pl.ds(pos, count)])
        hi[pl.ds(slot * OWN + pos, count)] = h
        lo[pl.ds(slot * OWN + pos, count)] = l

    def convert_all(slot):
        def step(u, carry):
            convert(slot, u * CH, CH)
            return carry

        lax.fori_loop(0, STEPS, step, 0)

    hi[ZERO] = jnp.zeros((BS, BS), jnp.bfloat16)
    lo[ZERO] = jnp.zeros((BS, BS), jnp.bfloat16)
    load.wait()
    convert_all(NEAR)

    for m in range(len(offsets)):
        col_copy(m).wait()
    row_in_tile = lax.broadcasted_iota(jnp.int32, (8, 128), 0)
    own_tile = wcols[NEAR]
    for i in range(RB):
        own_cols = jnp.broadcast_to(own_tile[i : i + 1, :], (8, 128))

        def slot_table(s, carry):
            tile = wcols[s]
            found = jnp.full((8, 128), ZERO, jnp.int32)
            first = (s * RB + row_in_tile) * NNZ
            for t in range(NNZ):
                col = jnp.broadcast_to(tile[:, t : t + 1], (8, 128))
                found = jnp.where(col == own_cols, first + t, found)
            tab_v[pl.ds(pl.multiple_of(i * TROWS + s * 8, 8), 8), :] = jnp.where(
                row_in_tile < RB, found, ZERO
            )
            return carry

        lax.fori_loop(0, SLOTS, slot_table, 0)
    lane = lax.broadcasted_iota(jnp.int32, (8, 128), 1)
    coef = jnp.full((8, 128), ZERO, jnp.int32)
    for a in range(NNZ):
        col = jnp.broadcast_to(own_tile[:, a : a + 1], (8, 128))
        coef = jnp.where(col == lane + base, NEAR * OWN + row_in_tile * NNZ + a, coef)
    tab_v[RB * TROWS : RB * TROWS + 8, :] = jnp.where(row_in_tile < RB, coef, ZERO)
    to_smem = pltpu.make_async_copy(tab_v, tab, s_local.at[1])
    to_smem.start()
    to_smem.wait()

    def fwd_from_left(u):
        pos = at_right(u)
        return remote(
            win.at[1, pl.ds(pos, CH)],
            win.at[2 * p, pl.ds(pos, CH)],
            s_fwd.at[0, u],
            r_fwd.at[0, u],
            partner,
        )

    def fwd_from_right(u):
        pos = at_left(u)
        return remote(
            win.at[5, pl.ds(pos, CH)],
            win.at[4 + 2 * p, pl.ds(pos, CH)],
            s_fwd.at[1, u],
            r_fwd.at[1, u],
            partner,
        )

    def fwd_far(u):
        pos = at_right(u) * p + at_left(u) * (1 - p)
        return remote(
            win.at[5 - 4 * p, pl.ds(pos, CH)],
            win.at[6 - 6 * p, pl.ds(pos, CH)],
            s_fwd.at[2, u],
            r_fwd.at[2, u],
            far_dev,
        )

    def take_partner(u):
        fwd_from_left(u).wait_recv()
        convert(2 - 2 * p, at_right(u), CH)
        fwd_from_right(u).wait_recv()
        convert(6 - 2 * p, at_left(u), CH)

    part_copy().wait_recv()
    convert_all(4 - 2 * p)

    def near_step(u, carry):
        own_right(u).wait_recv()
        own_left(u).wait_recv()
        fwd_from_left(u).start()
        fwd_from_right(u).start()
        fwd_far(u).start()
        convert(1, at_right(u), CH)
        convert(5, at_left(u), CH)
        take_partner(u)
        return carry

    lax.fori_loop(0, STEPS, near_step, 0)

    def tile(ref, index, count_a):
        return jnp.concatenate(
            [
                jnp.concatenate([ref[index[a][b]] for b in range(QB)], axis=1)
                for a in range(count_a)
            ],
            axis=0,
        )

    def window_rows(i):
        rows = []
        for a in range(NNZ):
            r = jnp.clip(cols[i, a] - base, 0, SLOTS * RB - 1)
            rows.append((r, i * TROWS + r + lax.shift_left(lax.shift_right_logical(r, 2), 2)))
        return rows

    def part(q):
        return pl.ds(pl.multiple_of(q * QB * BS, QB * BS), QB * BS)

    def near_square(i, carry):
        rows = window_rows(i)

        def columns(q, carry):
            index = []
            for r, row in rows:
                in_far = jnp.logical_and(r >= far * RB, r < far * RB + RB)
                index.append(
                    [jnp.where(in_far, ZERO, tab[row, q * QB + b]) for b in range(QB)]
                )
            own = NEAR * OWN + i * NNZ
            lhs_hi = jnp.concatenate([hi[own + a] for a in range(NNZ)], axis=1)
            lhs_lo = jnp.concatenate([lo[own + a] for a in range(NNZ)], axis=1)
            sq[i, :, part(q)] = dot3(
                lhs_hi, lhs_lo, tile(hi, index, NNZ), tile(lo, index, NNZ)
            )
            return carry

        lax.fori_loop(0, NNZ // QB, columns, 0)
        return carry

    lax.fori_loop(0, RB, near_square, 0)

    def far_square(i, j):
        at = tab[RB * TROWS + i, far * RB + j]
        lhs_hi, lhs_lo = hi[at], lo[at]

        def columns(q, carry):
            index = [[tab[i * TROWS + far * 8 + j, q * QB + b] for b in range(QB)]]
            sq[i, :, part(q)] += dot3(lhs_hi, lhs_lo, tile(hi, index, 1), tile(lo, index, 1))
            return carry

        lax.fori_loop(0, NNZ // QB, columns, 0)

    def out_copy(i):
        rows = pl.ds(i * NNZ, NNZ)
        return pltpu.make_async_copy(win.at[NEAR, rows], out_ref.at[rows], s_local.at[2 + i])

    def cube(i):
        h, l = split(sq[i])
        sq_hi[...] = h
        sq_lo[...] = l
        rows = window_rows(i)

        def columns(q, carry):
            index = [[tab[row, q * QB + b] for b in range(QB)] for _, row in rows]
            third = dot3(sq_hi[...], sq_lo[...], tile(hi, index, NNZ), tile(lo, index, NNZ))
            res = 3.0 * sq[i, :, part(q)] - 2.0 * third
            for b in range(QB):
                win[NEAR, i * NNZ + q * QB + b] = res[:, b * BS : (b + 1) * BS]
            return carry

        lax.fori_loop(0, NNZ // QB, columns, 0)
        out_copy(i).start()

    def far_step(t, carry):
        j = (RB - 1 - t) * (1 - p) + t * p
        for half in range(2):
            u = 2 * t + half
            pos = at_right(u) * (1 - p) + at_left(u) * p
            fwd_far(u).wait_recv()
            convert(far, pos, CH)

        def row(m, carry):
            far_square(m * (1 - p) + (RB - 1 - m) * p, j)
            return carry

        lax.fori_loop(0, RB - t, row, 0)
        last = RB - 1 - t
        cube(last * (1 - p) + (RB - 1 - last) * p)
        return carry

    lax.fori_loop(0, RB, far_step, 0)

    def finish(u, carry):
        own_right(u).wait_send()
        own_left(u).wait_send()
        fwd_from_left(u).wait_send()
        fwd_from_right(u).wait_send()
        fwd_far(u).wait_send()
        return carry

    lax.fori_loop(0, STEPS, finish, 0)
    part_copy().wait_send()
    for i in range(RB):
        out_copy(i).wait()


X = 24
CAP = 68
PCH = 4
PSTEPS = CAP // PCH
ASTEPS = OWN // PCH
ESTEPS = (OWN + NNZ) // PCH
PART0, RAW_A0, RAW_B0, POOL_A0, POOL_B0 = 48, 96, 144, 192, 192 + CAP
NONE = POOL_B0 + OWN
AHEAD = 3
ROUNDS = 7
KEEP = 8
PAD = -100000


def fast_kernel(
    n,
    x_ref,
    colv_ref,
    cols,
    out_ref,
    flag_ref,
    own,
    part,
    raw_a,
    raw_b,
    pool_a,
    pool_b,
    pool_out,
    hi,
    lo,
    sq,
    sq_hi,
    sq_lo,
    colbuf,
    wcols,
    mapbuf,
    maps,
    inv_v,
    inv,
    tab_v,
    tab,
    idx,
    fbuf,
    fin,
    s_cols,
    r_cols,
    s_map,
    r_map,
    s_raw,
    r_raw,
    s_pool,
    r_pool,
    s_fraw,
    r_fraw,
    s_fpool,
    r_fpool,
    s_part,
    r_part,
    s_flag,
    r_flag,
    s_local,
):
    f32, i32 = jnp.float32, jnp.int32
    d = lax.axis_index("grid")
    p = lax.rem(d, 2)
    s = 2 * p - 1
    base = RB * (d - NEAR)
    offsets = (-3, -2, -1, 1, 2, 3)

    def at(off):
        return lax.rem(d + n + off, n)

    def flip(r):
        bit = 1 << r if isinstance(r, int) else 16 + (r - 4) * 16 + jnp.maximum(r - 5, 0) * 16
        return d + bit - 2 * bit * lax.rem(d // bit, 2)

    ahead, ahead2, partner = at(s), at(2 * s), at(-s)

    barrier = pltpu.get_barrier_semaphore()
    greeted = [at(off) for off in offsets] + [flip(r) for r in range(2, ROUNDS)]
    for dev in greeted:
        pl.semaphore_signal(barrier, inc=1, device_id=(dev,), device_id_type=MESH)
    load = pltpu.make_async_copy(x_ref, own, s_local.at[0])
    load.start()
    colbuf[...] = jnp.full((8, 128), PAD, i32)
    colbuf[0:RB, 0:NNZ] = colv_ref[...]
    wcols[NEAR] = colbuf[...]
    pl.semaphore_wait(barrier, len(greeted))

    def remote(src, dst, send, recv, dev):
        return pltpu.make_async_remote_copy(
            src_ref=src,
            dst_ref=dst,
            send_sem=send,
            recv_sem=recv,
            device_id=(dev,),
            device_id_type=MESH,
        )

    def col_copy(m):
        off = offsets[m]
        return remote(colbuf, wcols.at[NEAR - off], s_cols.at[m], r_cols.at[m], at(off))

    def part_copy():
        return remote(x_ref, part, s_part.at[0], r_part.at[0], partner)

    def raw_copy(u):
        rows = pl.ds(u * CH, CH)
        return remote(x_ref.at[rows], raw_a.at[rows], s_raw.at[u], r_raw.at[u], ahead)

    def raw_fwd(u):
        rows = pl.ds(u * CH, CH)
        return remote(raw_a.at[rows], raw_b.at[rows], s_fraw.at[u], r_fraw.at[u], partner)

    def pool_copy(u):
        rows = pl.ds(u * PCH, PCH)
        return remote(pool_out.at[rows], pool_a.at[rows], s_pool.at[u], r_pool.at[u], ahead)

    def pool_fwd(u):
        rows = pl.ds(u * PCH, PCH)
        return remote(pool_a.at[rows], pool_b.at[rows], s_fpool.at[u], r_fpool.at[u], partner)

    def map_copy(m):
        return remote(
            mapbuf, maps.at[m], s_map.at[m], r_map.at[m], ahead if m == 0 else ahead2
        )

    def flag_copy(r):
        return remote(fbuf.at[r], fin.at[r], s_flag.at[r], r_flag.at[r], flip(r))

    def finish_round(r):
        flag_copy(r).wait_recv()
        fbuf[r + 1] = jnp.maximum(fbuf[r], fin[r])

    for m in range(len(offsets)):
        col_copy(m).start()

    def start_raw(u, carry):
        raw_copy(u).start()
        return carry

    lax.fori_loop(0, AHEAD, start_raw, 0)
    part_copy().start()

    def convert(ref, first, pos, count):
        h, l = split(ref[pl.ds(pos, count)])
        hi[pl.ds(first + pos, count)] = h
        lo[pl.ds(first + pos, count)] = l

    def convert_all(ref, first):
        def step(u, carry):
            convert(ref, first, u * CH, CH)
            return carry

        lax.fori_loop(0, STEPS, step, 0)

    hi[NONE] = jnp.zeros((BS, BS), jnp.bfloat16)
    lo[NONE] = jnp.zeros((BS, BS), jnp.bfloat16)

    for m in range(len(offsets)):
        col_copy(m).wait_recv()
    sub = lax.broadcasted_iota(i32, (8, 128), 0)
    lane = lax.broadcasted_iota(i32, (8, 128), 1)
    lane_col = lane + (RB * d - 64)

    def spread(tile, value):
        where = jnp.zeros((8, 128), f32)
        what = jnp.zeros((8, 128), i32)
        for t in range(NNZ):
            hit = jnp.broadcast_to(tile[:, t : t + 1], (8, 128)) == lane_col
            where = jnp.where(hit, 1.0, where)
            if value is not None:
                what = jnp.where(hit, value + t, what)
        return where, what

    next1, _ = spread(wcols[NEAR + s], None)
    next2, _ = spread(wcols[NEAR + 2 * s], None)

    def needed(readers, back):
        need = jnp.zeros((8, 128), f32)
        for j in range(RB):
            here = lane == 64 - RB * back * s + j
            row = jnp.zeros((1, 128), f32)
            for reader in readers:
                reads = jnp.max(jnp.where(here, reader, 0.0), axis=1, keepdims=True)
                row = jnp.maximum(row, jnp.max(reader * reads, axis=0, keepdims=True))
            need = jnp.where(sub == j, jnp.broadcast_to(row, (8, 128)), need)
        return need

    has_1, src_1 = spread(wcols[NEAR - s], sub * NNZ)
    has_2, src_2 = spread(wcols[NEAR - 2 * s], sub * NNZ + OWN)
    chosen = jnp.concatenate(
        [has_1 * needed([next1, next2], 1), has_2 * needed([next1], 2)], axis=0
    )
    square_row = lax.broadcasted_iota(i32, (128, 128), 0)
    square_lane = lax.broadcasted_iota(i32, (128, 128), 1)
    before = jnp.where(square_row < square_lane, 1.0, 0.0).astype(jnp.bfloat16)
    rank = jnp.dot(chosen.astype(jnp.bfloat16), before, preferred_element_type=f32)
    totals = jnp.sum(chosen, axis=1, keepdims=True)
    sub16 = lax.broadcasted_iota(i32, (16, 128), 0)
    count_1 = jnp.zeros((1, 1), f32)
    count_2 = jnp.zeros((1, 1), f32)
    for j in range(RB):
        count_1 = count_1 + totals[j : j + 1, :]
        count_2 = count_2 + totals[8 + j : 9 + j, :]
    start_2 = jnp.maximum(count_1, float(X))
    for r in range(RB):
        rank = rank + jnp.where(
            jnp.logical_and(sub16 > r, sub16 < 8),
            jnp.broadcast_to(totals[r : r + 1, :], (16, 128)),
            0.0,
        )
        rank = rank + jnp.where(
            jnp.logical_and(sub16 >= 8, s * (sub16 - 8 - r) < 0),
            jnp.broadcast_to(totals[8 + r : 9 + r, :], (16, 128)),
            0.0,
        )
    rank = rank + jnp.where(sub16 >= 8, jnp.broadcast_to(start_2, (16, 128)), 0.0)
    taken = jnp.logical_and(chosen > 0.5, rank < CAP - 0.5)
    slot = jnp.where(taken, rank, -1.0)
    slot_int = slot.astype(i32)
    mapbuf[...] = slot_int
    for m in range(2):
        map_copy(m).start()
    over = jnp.where(start_2 + count_2 > CAP + 0.5, 1.0, 0.0)
    fbuf[0] = jnp.broadcast_to(over, (8, 128))

    for tile in range(-(-CAP // 8)):
        found = jnp.zeros((8, 128), i32)
        for r in range(RB):
            hit = jnp.broadcast_to(slot_int[r : r + 1, :], (8, 128)) == sub + 8 * tile
            found = jnp.where(hit, jnp.broadcast_to(src_1[r : r + 1, :], (8, 128)), found)
            if tile * 8 >= X:
                hit = jnp.broadcast_to(slot_int[8 + r : 9 + r, :], (8, 128)) == sub + 8 * tile
                found = jnp.where(hit, jnp.broadcast_to(src_2[r : r + 1, :], (8, 128)), found)
        source = jnp.sum(found.astype(f32), axis=1, keepdims=True).astype(i32)
        inv_v[tile * 8 : tile * 8 + 8, :] = jnp.broadcast_to(source, (8, 128))
    to_inv = pltpu.make_async_copy(inv_v, inv, s_local.at[1])
    to_inv.start()
    to_inv.wait()

    part_copy().wait_recv()

    def pack_first(u, carry):
        for b in range(PCH):
            pool_out[u * PCH + b] = part[jnp.clip(inv[u * PCH + b, 0], 0, OWN - 1)]
        return carry

    lax.fori_loop(0, X // PCH, pack_first, 0)
    load.wait()
    convert_all(own, 0)
    convert_all(part, PART0)

    def lane_base(o):
        back = jnp.where(o >= 2, s, jnp.where(o <= -3, -2 * s, 0))
        return RB * (d + back) - 64

    def resolve(m, carry):
        i = m // NNZ
        r = jnp.clip(cols[i, lax.rem(m, NNZ)] - base, 0, SLOTS * RB - 1)
        w = lax.shift_right_logical(r, 2)
        row = w * 8 + lax.bitwise_and(r, 3)
        first = lane_base(s * (w - NEAR))
        for b in range(NNZ):
            found = tab[row, jnp.clip(cols[i, b] - first, 0, 127)]
            idx[m * NNZ + b] = jnp.clip(found, 0, NONE)
        return carry

    def take_raw_b(u):
        raw_fwd(u).wait_recv()
        convert(raw_b, RAW_B0, u * CH, CH)

    def build_table():
        for m in range(2):
            map_copy(m).wait_recv()

        def put(o, tile):
            at_row = pl.multiple_of((NEAR + s * o) * 8, 8)
            tab_v[pl.ds(at_row, 8), :] = jnp.where(sub < RB, jnp.clip(tile, 0, NONE), NONE)

        for o, first in ((0, 0), (-1, PART0), (1, RAW_A0), (-2, RAW_B0)):
            has, where = spread(wcols[NEAR + s * o], sub * NNZ + first)
            put(o, jnp.where(has > 0.5, where, NONE))
        for o, m, half, first in ((2, 0, 0, POOL_A0), (3, 0, 8, POOL_A0), (-3, 1, 0, POOL_B0)):
            got = maps[m, half : half + 8, :]
            put(o, jnp.where(got >= 0, got + first, NONE))
        to_tab = pltpu.make_async_copy(tab_v, tab, s_local.at[1])
        to_tab.start()
        to_tab.wait()

    for u in range(STEPS):
        raw_copy(u).wait_recv()
        raw_fwd(u).start()
        if u % 2 == 0:
            if u > 0:
                finish_round(u // 2 - 1)
            flag_copy(u // 2).start()
        if u + AHEAD < STEPS:
            raw_copy(u + AHEAD).start()
        else:
            pool_copy(u + AHEAD - STEPS).start()
        convert(raw_a, RAW_A0, u * CH, CH)
        if u > 0:
            take_raw_b(u - 1)
        if u == 3:
            build_table()
    take_raw_b(STEPS - 1)

    def pack_rest(u, carry):
        for b in range(PCH):
            source = inv[u * PCH + b, 0]
            pool_out[u * PCH + b] = jnp.where(
                source < OWN,
                part[jnp.clip(source, 0, OWN - 1)],
                raw_b[jnp.clip(source - OWN, 0, OWN - 1)],
            )
        pool_copy(u).start()
        return carry

    def take_pool_b(u):
        pool_fwd(u).wait_recv()
        convert(pool_b, POOL_B0, u * PCH, PCH)

    def pool_step(u, carry):
        pool_copy(u).wait_recv()
        pool_fwd(u).start()

        @pl.when(u + AHEAD < X // PCH)
        def _():
            pool_copy(u + AHEAD).start()

        @pl.when(u + AHEAD >= X // PCH)
        def _():
            pack_rest(u + AHEAD, 0)

        convert(pool_a, POOL_A0, u * PCH, PCH)

        @pl.when(u > 0)
        def _():
            take_pool_b(u - 1)

        lax.fori_loop(u * RB, (u + 1) * RB, resolve, 0)
        return carry

    finish_round(STEPS // 2 - 1)
    lax.fori_loop(0, ASTEPS, pool_step, 0)
    lax.fori_loop(ASTEPS + AHEAD, PSTEPS, pack_rest, 0)
    take_pool_b(ASTEPS - 1)

    def tile(ref, index, count_a):
        return jnp.concatenate(
            [
                jnp.concatenate([ref[index[a][b]] for b in range(QB)], axis=1)
                for a in range(count_a)
            ],
            axis=0,
        )

    def block_at(i, a, b):
        return jnp.clip(idx[(i * NNZ + a) * NNZ + b], 0, NONE)

    def part_of(q):
        return pl.ds(q * QB * BS, QB * BS)

    def near_square(i, carry):
        keep = []
        for a in range(NNZ):
            r = jnp.clip(cols[i, a] - base, 0, SLOTS * RB - 1)
            keep.append(s * (lax.shift_right_logical(r, 2) - NEAR) < 3)
        lhs_hi = jnp.concatenate([hi[i * NNZ + a] for a in range(NNZ)], axis=1)
        lhs_lo = jnp.concatenate([lo[i * NNZ + a] for a in range(NNZ)], axis=1)
        for q in range(NNZ // QB):
            index = [
                [
                    jnp.where(keep[a], block_at(i, a, q * QB + b), NONE)
                    for b in range(QB)
                ]
                for a in range(NNZ)
            ]
            sq[i, :, part_of(q)] = dot3(
                lhs_hi, lhs_lo, tile(hi, index, NNZ), tile(lo, index, NNZ)
            )
        return carry

    lax.fori_loop(0, RB, near_square, 0)

    def last_pool(u, carry):
        pool_copy(u).wait_recv()
        convert(pool_a, POOL_A0, u * PCH, PCH)
        return carry

    lax.fori_loop(ASTEPS, ESTEPS, last_pool, 0)

    far_base = lane_base(3)

    def out_copy(i):
        rows = pl.ds(i * NNZ, NNZ)
        return pltpu.make_async_copy(own.at[rows], out_ref.at[rows], s_local.at[2 + i])

    def turn(t):
        return t * p + (RB - 1 - t) * (1 - p)

    def finish_row(t, count):
        i = turn(t)
        coef = [
            jnp.clip(tab[NEAR * 8 + i, 64 + 3 * RB * s + turn(u)], 0, NONE)
            for u in range(count)
        ]
        lhs_hi = jnp.concatenate([hi[c] for c in coef], axis=1)
        lhs_lo = jnp.concatenate([lo[c] for c in coef], axis=1)
        lanes = [jnp.clip(cols[i, b] - far_base, 0, 127) for b in range(NNZ)]
        for q in range(NNZ // QB):
            index = [
                [
                    jnp.clip(tab[(NEAR + 3 * s) * 8 + turn(u), lanes[q * QB + b]], 0, NONE)
                    for b in range(QB)
                ]
                for u in range(count)
            ]
            sq[i, :, part_of(q)] += dot3(
                lhs_hi, lhs_lo, tile(hi, index, count), tile(lo, index, count)
            )
        h, l = split(sq[i])
        sq_hi[...] = h
        sq_lo[...] = l
        for q in range(NNZ // QB):
            index = [
                [block_at(i, a, q * QB + b) for b in range(QB)]
                for a in range(NNZ)
            ]
            third = dot3(sq_hi[...], sq_lo[...], tile(hi, index, NNZ), tile(lo, index, NNZ))
            res = 3.0 * sq[i, :, part_of(q)] - 2.0 * third
            for b in range(QB):
                own[i * NNZ + q * QB + b] = res[:, b * BS : (b + 1) * BS]
        out_copy(i).start()

    def late_row(t, carry):
        r = STEPS // 2 - 1 + t
        flag_copy(r).start()
        finish_row(t, RB)
        finish_round(r)
        return carry

    finish_row(0, 1)
    lax.fori_loop(ESTEPS, PSTEPS, last_pool, 0)
    lax.fori_loop(1, RB, late_row, 0)
    flag_ref[0, 0] = jnp.max(fbuf[ROUNDS]).astype(i32)

    def done_raw(u, carry):
        raw_copy(u).wait_send()
        raw_fwd(u).wait_send()
        return carry

    def done_pool(u, carry):
        pool_copy(u).wait_send()
        return carry

    def done_fwd(u, carry):
        pool_fwd(u).wait_send()
        return carry

    lax.fori_loop(0, STEPS, done_raw, 0)
    lax.fori_loop(0, PSTEPS, done_pool, 0)
    lax.fori_loop(0, ASTEPS, done_fwd, 0)
    part_copy().wait_send()
    for m in range(len(offsets)):
        col_copy(m).wait_send()
    for m in range(2):
        map_copy(m).wait_send()
    for r in range(ROUNDS):
        flag_copy(r).wait_send()
    for i in range(RB):
        out_copy(i).wait()


def call_full(blocks, block_cols, n):
    dma = pltpu.SemaphoreType.DMA
    return pl.pallas_call(
        functools.partial(full_kernel, n),
        out_shape=jax.ShapeDtypeStruct((OWN, BS, BS), jnp.float32),
        in_specs=[
            pl.BlockSpec(memory_space=pl.ANY),
            pl.BlockSpec(memory_space=pltpu.VMEM),
            pl.BlockSpec(memory_space=pltpu.SMEM),
        ],
        out_specs=pl.BlockSpec(memory_space=pl.ANY),
        scratch_shapes=[
            pltpu.VMEM((SLOTS, OWN, BS, BS), jnp.float32),
            pltpu.VMEM((ZERO + 1, BS, BS), jnp.bfloat16),
            pltpu.VMEM((ZERO + 1, BS, BS), jnp.bfloat16),
            pltpu.VMEM((RB, BS, NNZ * BS), jnp.float32),
            pltpu.VMEM((BS, NNZ * BS), jnp.bfloat16),
            pltpu.VMEM((BS, NNZ * BS), jnp.bfloat16),
            pltpu.VMEM((8, 128), jnp.int32),
            pltpu.VMEM((SLOTS, 8, 128), jnp.int32),
            pltpu.VMEM((RB * TROWS + 8, 128), jnp.int32),
            pltpu.SMEM((RB * TROWS + 8, 128), jnp.int32),
            dma((6,)),
            dma((6,)),
            dma((2, STEPS)),
            dma((2, STEPS)),
            dma((3, STEPS)),
            dma((3, STEPS)),
            dma((1,)),
            dma((1,)),
            dma((2 + RB,)),
        ],
        compiler_params=pltpu.CompilerParams(
            collective_id=1, has_side_effects=True, vmem_limit_bytes=58 << 20
        ),
        name="mcweeny_full",
    )(blocks, block_cols, block_cols)


def call_fast(blocks, block_cols, n):
    dma = pltpu.SemaphoreType.DMA
    buffer = lambda count: pltpu.VMEM((count, BS, BS), jnp.float32)
    half = pltpu.VMEM((NONE + 1, BS, BS), jnp.bfloat16)
    rows = -(-CAP // 8) * 8
    return pl.pallas_call(
        functools.partial(fast_kernel, n),
        out_shape=[
            jax.ShapeDtypeStruct((OWN, BS, BS), jnp.float32),
            jax.ShapeDtypeStruct((1, 1), jnp.int32),
        ],
        in_specs=[
            pl.BlockSpec(memory_space=pl.ANY),
            pl.BlockSpec(memory_space=pltpu.VMEM),
            pl.BlockSpec(memory_space=pltpu.SMEM),
        ],
        out_specs=[
            pl.BlockSpec(memory_space=pl.ANY),
            pl.BlockSpec(memory_space=pltpu.SMEM),
        ],
        scratch_shapes=[
            buffer(OWN),
            buffer(OWN),
            buffer(OWN),
            buffer(OWN),
            buffer(CAP),
            buffer(OWN),
            buffer(CAP),
            half,
            half,
            pltpu.VMEM((RB, BS, NNZ * BS), jnp.float32),
            pltpu.VMEM((BS, NNZ * BS), jnp.bfloat16),
            pltpu.VMEM((BS, NNZ * BS), jnp.bfloat16),
            pltpu.VMEM((8, 128), jnp.int32),
            pltpu.VMEM((SLOTS, 8, 128), jnp.int32),
            pltpu.VMEM((16, 128), jnp.int32),
            pltpu.VMEM((2, 16, 128), jnp.int32),
            pltpu.VMEM((rows, 128), jnp.int32),
            pltpu.SMEM((rows, 128), jnp.int32),
            pltpu.VMEM((TROWS, 128), jnp.int32),
            pltpu.SMEM((TROWS, 128), jnp.int32),
            pltpu.SMEM((OWN * NNZ,), jnp.int32),
            pltpu.VMEM((ROUNDS + 1, 8, 128), jnp.float32),
            pltpu.VMEM((ROUNDS, 8, 128), jnp.float32),
            dma((6,)),
            dma((6,)),
            dma((2,)),
            dma((2,)),
            dma((STEPS,)),
            dma((STEPS,)),
            dma((PSTEPS,)),
            dma((PSTEPS,)),
            dma((STEPS,)),
            dma((STEPS,)),
            dma((ASTEPS,)),
            dma((ASTEPS,)),
            dma((1,)),
            dma((1,)),
            dma((ROUNDS,)),
            dma((ROUNDS,)),
            dma((2 + RB,)),
        ],
        compiler_params=pltpu.CompilerParams(
            collective_id=0, has_side_effects=True, vmem_limit_bytes=58 << 20
        ),
        name="mcweeny_fast",
    )(blocks, block_cols, block_cols)


def keep_kernel(src, dst, buf, got, put):
    parts = range(KEEP)
    rows = [pl.ds(i * (OWN // KEEP), OWN // KEEP) for i in parts]
    loads = [pltpu.make_async_copy(src.at[rows[i]], buf.at[rows[i]], got.at[i]) for i in parts]
    stores = [pltpu.make_async_copy(buf.at[rows[i]], dst.at[rows[i]], put.at[i]) for i in parts]
    for load in loads:
        load.start()
    for load, store in zip(loads, stores):
        load.wait()
        store.start()
    for store in stores:
        store.wait()


def keep(blocks):
    dma = pltpu.SemaphoreType.DMA
    return pl.pallas_call(
        keep_kernel,
        out_shape=jax.ShapeDtypeStruct(blocks.shape, blocks.dtype),
        in_specs=[pl.BlockSpec(memory_space=pl.ANY)],
        out_specs=pl.BlockSpec(memory_space=pl.ANY),
        scratch_shapes=[
            pltpu.VMEM((OWN, BS, BS), jnp.float32),
            dma((KEEP,)),
            dma((KEEP,)),
        ],
        compiler_params=pltpu.CompilerParams(vmem_limit_bytes=58 << 20),
        name="keep",
    )(blocks)


def body(density_blocks, block_cols, n):
    blocks = density_blocks.reshape(OWN, BS, BS)
    out, over = call_fast(blocks, block_cols, n)
    out = lax.cond(
        over[0, 0] > 0,
        lambda b, c, o: call_full(b, c, n),
        lambda b, c, o: o,
        blocks,
        block_cols,
        out,
    )
    return keep(out).reshape(RB, NNZ, BS, BS)


def solution(mesh):
    placed = (P("grid", None, None, None), P("grid", None))
    return jax.shard_map(
        functools.partial(body, n=mesh.shape["grid"]),
        mesh=mesh,
        in_specs=placed,
        out_specs=P("grid", None, None, None),
        check_vma=False,
    )
```

```python
import functools

import jax
import jax.numpy as jnp
from jax import lax
from jax.experimental import pallas as pl
from jax.experimental.pallas import tpu as pltpu
from jax.sharding import PartitionSpec as P

MESH = pl.DeviceIdType.MESH
BS = 128
NNZ = 12
NEAR = 3
RB = 4
OWN = RB * NNZ
SLOTS = 2 * NEAR + 1
ZERO = SLOTS * OWN
STEPS = 8
CH = OWN // STEPS
QB = 4
TROWS = SLOTS * 8


def split(x):
    high = x.astype(jnp.bfloat16)
    return high, (x - high.astype(jnp.float32)).astype(jnp.bfloat16)


def dot3(lhs_hi, lhs_lo, rhs_hi, rhs_lo):
    dot = functools.partial(jnp.dot, preferred_element_type=jnp.float32)
    return dot(lhs_hi, rhs_hi) + dot(lhs_lo, rhs_hi) + dot(lhs_hi, rhs_lo)


def full_kernel(
    n,
    x_ref,
    colv_ref,
    cols,
    out_ref,
    win,
    hi,
    lo,
    sq,
    sq_hi,
    sq_lo,
    colbuf,
    wcols,
    tab_v,
    tab,
    s_cols,
    r_cols,
    s_own,
    r_own,
    s_fwd,
    r_fwd,
    s_part,
    r_part,
    s_local,
):
    d = lax.axis_index("grid")
    p = lax.rem(d, 2)
    right, left = lax.rem(d + 2, n), lax.rem(d + n - 2, n)
    partner = d + 1 - 2 * p
    far_dev = lax.rem(d + n - 1 + 2 * p, n)
    far = 6 * p
    base = RB * (d - NEAR)
    offsets = (-3, -2, -1, 1, 2, 3)

    barrier = pltpu.get_barrier_semaphore()
    for off in offsets:
        pl.semaphore_signal(
            barrier, inc=1, device_id=(lax.rem(d + n + off, n),), device_id_type=MESH
        )
    load = pltpu.make_async_copy(x_ref, win.at[NEAR], s_local.at[0])
    load.start()
    colbuf[...] = jnp.full((8, 128), -1, jnp.int32)
    colbuf[0:RB, 0:NNZ] = colv_ref[...]
    wcols[NEAR] = colbuf[...]
    pl.semaphore_wait(barrier, len(offsets))

    def remote(src, dst, send, recv, dev):
        return pltpu.make_async_remote_copy(
            src_ref=src,
            dst_ref=dst,
            send_sem=send,
            recv_sem=recv,
            device_id=(dev,),
            device_id_type=MESH,
        )

    def col_copy(m):
        off = offsets[m]
        return remote(
            colbuf,
            wcols.at[NEAR - off],
            s_cols.at[m],
            r_cols.at[m],
            lax.rem(d + n + off, n),
        )

    for m in range(len(offsets)):
        col_copy(m).start()

    def at_right(u):
        return (RB - 1 - u // 2) * NNZ + lax.rem(u, 2) * CH

    def at_left(u):
        return (u // 2) * NNZ + lax.rem(u, 2) * CH

    def own_right(u):
        pos = at_right(u)
        return remote(
            x_ref.at[pl.ds(pos, CH)],
            win.at[1, pl.ds(pos, CH)],
            s_own.at[0, u],
            r_own.at[0, u],
            right,
        )

    def own_left(u):
        pos = at_left(u)
        return remote(
            x_ref.at[pl.ds(pos, CH)],
            win.at[5, pl.ds(pos, CH)],
            s_own.at[1, u],
            r_own.at[1, u],
            left,
        )

    def part_copy():
        return remote(
            x_ref, win.at[2 + 2 * p], s_part.at[0], r_part.at[0], partner
        )

    def start_own(u, carry):
        own_right(u).start()
        own_left(u).start()
        return carry

    lax.fori_loop(0, STEPS, start_own, 0)
    part_copy().start()

    def convert(slot, pos, count):
        h, l = split(win[slot, pl.ds(pos, count)])
        hi[pl.ds(slot * OWN + pos, count)] = h
        lo[pl.ds(slot * OWN + pos, count)] = l

    def convert_all(slot):
        def step(u, carry):
            convert(slot, u * CH, CH)
            return carry

        lax.fori_loop(0, STEPS, step, 0)

    hi[ZERO] = jnp.zeros((BS, BS), jnp.bfloat16)
    lo[ZERO] = jnp.zeros((BS, BS), jnp.bfloat16)
    load.wait()
    convert_all(NEAR)

    for m in range(len(offsets)):
        col_copy(m).wait()
    row_in_tile = lax.broadcasted_iota(jnp.int32, (8, 128), 0)
    own_tile = wcols[NEAR]
    for i in range(RB):
        own_cols = jnp.broadcast_to(own_tile[i : i + 1, :], (8, 128))

        def slot_table(s, carry):
            tile = wcols[s]
            found = jnp.full((8, 128), ZERO, jnp.int32)
            first = (s * RB + row_in_tile) * NNZ
            for t in range(NNZ):
                col = jnp.broadcast_to(tile[:, t : t + 1], (8, 128))
                found = jnp.where(col == own_cols, first + t, found)
            tab_v[pl.ds(pl.multiple_of(i * TROWS + s * 8, 8), 8), :] = jnp.where(
                row_in_tile < RB, found, ZERO
            )
            return carry

        lax.fori_loop(0, SLOTS, slot_table, 0)
    lane = lax.broadcasted_iota(jnp.int32, (8, 128), 1)
    coef = jnp.full((8, 128), ZERO, jnp.int32)
    for a in range(NNZ):
        col = jnp.broadcast_to(own_tile[:, a : a + 1], (8, 128))
        coef = jnp.where(col == lane + base, NEAR * OWN + row_in_tile * NNZ + a, coef)
    tab_v[RB * TROWS : RB * TROWS + 8, :] = jnp.where(row_in_tile < RB, coef, ZERO)
    to_smem = pltpu.make_async_copy(tab_v, tab, s_local.at[1])
    to_smem.start()
    to_smem.wait()

    def fwd_from_left(u):
        pos = at_right(u)
        return remote(
            win.at[1, pl.ds(pos, CH)],
            win.at[2 * p, pl.ds(pos, CH)],
            s_fwd.at[0, u],
            r_fwd.at[0, u],
            partner,
        )

    def fwd_from_right(u):
        pos = at_left(u)
        return remote(
            win.at[5, pl.ds(pos, CH)],
            win.at[4 + 2 * p, pl.ds(pos, CH)],
            s_fwd.at[1, u],
            r_fwd.at[1, u],
            partner,
        )

    def fwd_far(u):
        pos = at_right(u) * p + at_left(u) * (1 - p)
        return remote(
            win.at[5 - 4 * p, pl.ds(pos, CH)],
            win.at[6 - 6 * p, pl.ds(pos, CH)],
            s_fwd.at[2, u],
            r_fwd.at[2, u],
            far_dev,
        )

    def take_partner(u):
        fwd_from_left(u).wait_recv()
        convert(2 - 2 * p, at_right(u), CH)
        fwd_from_right(u).wait_recv()
        convert(6 - 2 * p, at_left(u), CH)

    part_copy().wait_recv()
    convert_all(4 - 2 * p)

    def near_step(u, carry):
        own_right(u).wait_recv()
        own_left(u).wait_recv()
        fwd_from_left(u).start()
        fwd_from_right(u).start()
        fwd_far(u).start()
        convert(1, at_right(u), CH)
        convert(5, at_left(u), CH)
        take_partner(u)
        return carry

    lax.fori_loop(0, STEPS, near_step, 0)

    def tile(ref, index, count_a):
        return jnp.concatenate(
            [
                jnp.concatenate([ref[index[a][b]] for b in range(QB)], axis=1)
                for a in range(count_a)
            ],
            axis=0,
        )

    def window_rows(i):
        rows = []
        for a in range(NNZ):
            r = jnp.clip(cols[i, a] - base, 0, SLOTS * RB - 1)
            rows.append((r, i * TROWS + r + lax.shift_left(lax.shift_right_logical(r, 2), 2)))
        return rows

    def part(q):
        return pl.ds(pl.multiple_of(q * QB * BS, QB * BS), QB * BS)

    def near_square(i, carry):
        rows = window_rows(i)

        def columns(q, carry):
            index = []
            for r, row in rows:
                in_far = jnp.logical_and(r >= far * RB, r < far * RB + RB)
                index.append(
                    [jnp.where(in_far, ZERO, tab[row, q * QB + b]) for b in range(QB)]
                )
            own = NEAR * OWN + i * NNZ
            lhs_hi = jnp.concatenate([hi[own + a] for a in range(NNZ)], axis=1)
            lhs_lo = jnp.concatenate([lo[own + a] for a in range(NNZ)], axis=1)
            sq[i, :, part(q)] = dot3(
                lhs_hi, lhs_lo, tile(hi, index, NNZ), tile(lo, index, NNZ)
            )
            return carry

        lax.fori_loop(0, NNZ // QB, columns, 0)
        return carry

    lax.fori_loop(0, RB, near_square, 0)

    def far_square(i, j):
        at = tab[RB * TROWS + i, far * RB + j]
        lhs_hi, lhs_lo = hi[at], lo[at]

        def columns(q, carry):
            index = [[tab[i * TROWS + far * 8 + j, q * QB + b] for b in range(QB)]]
            sq[i, :, part(q)] += dot3(lhs_hi, lhs_lo, tile(hi, index, 1), tile(lo, index, 1))
            return carry

        lax.fori_loop(0, NNZ // QB, columns, 0)

    def out_copy(i):
        rows = pl.ds(i * NNZ, NNZ)
        return pltpu.make_async_copy(win.at[NEAR, rows], out_ref.at[rows], s_local.at[2 + i])

    def cube(i):
        h, l = split(sq[i])
        sq_hi[...] = h
        sq_lo[...] = l
        rows = window_rows(i)

        def columns(q, carry):
            index = [[tab[row, q * QB + b] for b in range(QB)] for _, row in rows]
            third = dot3(sq_hi[...], sq_lo[...], tile(hi, index, NNZ), tile(lo, index, NNZ))
            res = 3.0 * sq[i, :, part(q)] - 2.0 * third
            for b in range(QB):
                win[NEAR, i * NNZ + q * QB + b] = res[:, b * BS : (b + 1) * BS]
            return carry

        lax.fori_loop(0, NNZ // QB, columns, 0)
        out_copy(i).start()

    def far_step(t, carry):
        j = (RB - 1 - t) * (1 - p) + t * p
        for half in range(2):
            u = 2 * t + half
            pos = at_right(u) * (1 - p) + at_left(u) * p
            fwd_far(u).wait_recv()
            convert(far, pos, CH)

        def row(m, carry):
            far_square(m * (1 - p) + (RB - 1 - m) * p, j)
            return carry

        lax.fori_loop(0, RB - t, row, 0)
        last = RB - 1 - t
        cube(last * (1 - p) + (RB - 1 - last) * p)
        return carry

    lax.fori_loop(0, RB, far_step, 0)

    def finish(u, carry):
        own_right(u).wait_send()
        own_left(u).wait_send()
        fwd_from_left(u).wait_send()
        fwd_from_right(u).wait_send()
        fwd_far(u).wait_send()
        return carry

    lax.fori_loop(0, STEPS, finish, 0)
    part_copy().wait_send()
    for i in range(RB):
        out_copy(i).wait()


X = 24
CAP = 68
PCH = 4
PSTEPS = CAP // PCH
ASTEPS = OWN // PCH
ESTEPS = (OWN + NNZ) // PCH
PART0, RAW_A0, RAW_B0, POOL_A0, POOL_B0 = 48, 96, 144, 192, 192 + CAP
NONE = POOL_B0 + OWN
AHEAD = 3
ROUNDS = 4
GROUPS = 8
KEEP = 8
PAD = -100000


def fast_kernel(
    n,
    x_ref,
    colv_ref,
    cols,
    out_ref,
    flag_ref,
    own,
    part,
    raw_a,
    raw_b,
    pool_a,
    pool_b,
    pool_out,
    hi,
    lo,
    sq,
    sq_hi,
    sq_lo,
    colbuf,
    wcols,
    mapbuf,
    maps,
    inv_v,
    inv,
    tab_v,
    tab,
    idx,
    fbuf,
    fin,
    gin,
    s_cols,
    r_cols,
    s_map,
    r_map,
    s_raw,
    r_raw,
    s_pool,
    r_pool,
    s_fraw,
    r_fraw,
    s_fpool,
    r_fpool,
    s_part,
    r_part,
    s_flag,
    r_flag,
    s_group,
    r_group,
    s_local,
):
    f32, i32 = jnp.float32, jnp.int32
    d = lax.axis_index("grid")
    p = lax.rem(d, 2)
    s = 2 * p - 1
    base = RB * (d - NEAR)
    offsets = (-3, -2, -1, 1, 2, 3)

    def at(off):
        return lax.rem(d + n + off, n)

    def flip(change):
        to = d
        for r in range(7):
            if (change >> r) % 2:
                to = to + (1 << r) - (2 << r) * lax.rem(d // (1 << r), 2)
        return to

    ahead, ahead2, partner = at(s), at(2 * s), at(-s)

    barrier = pltpu.get_barrier_semaphore()
    greeted = [at(off) for off in offsets] + [flip(1 << r) for r in range(2, ROUNDS)]
    greeted = greeted + [flip(m << ROUNDS) for m in range(1, GROUPS)]
    for dev in greeted:
        pl.semaphore_signal(barrier, inc=1, device_id=(dev,), device_id_type=MESH)
    load = pltpu.make_async_copy(x_ref, own, s_local.at[0])
    load.start()
    colbuf[...] = jnp.full((8, 128), PAD, i32)
    colbuf[0:RB, 0:NNZ] = colv_ref[...]
    wcols[NEAR] = colbuf[...]
    pl.semaphore_wait(barrier, len(greeted))

    def remote(src, dst, send, recv, dev):
        return pltpu.make_async_remote_copy(
            src_ref=src,
            dst_ref=dst,
            send_sem=send,
            recv_sem=recv,
            device_id=(dev,),
            device_id_type=MESH,
        )

    def col_copy(m):
        off = offsets[m]
        return remote(colbuf, wcols.at[NEAR - off], s_cols.at[m], r_cols.at[m], at(off))

    def part_copy():
        return remote(x_ref, part, s_part.at[0], r_part.at[0], partner)

    def raw_copy(u):
        rows = pl.ds(u * CH, CH)
        return remote(x_ref.at[rows], raw_a.at[rows], s_raw.at[u], r_raw.at[u], ahead)

    def raw_fwd(u):
        rows = pl.ds(u * CH, CH)
        return remote(raw_a.at[rows], raw_b.at[rows], s_fraw.at[u], r_fraw.at[u], partner)

    def pool_copy(u):
        rows = pl.ds(u * PCH, PCH)
        return remote(pool_out.at[rows], pool_a.at[rows], s_pool.at[u], r_pool.at[u], ahead)

    def pool_fwd(u):
        rows = pl.ds(u * PCH, PCH)
        return remote(pool_a.at[rows], pool_b.at[rows], s_fpool.at[u], r_fpool.at[u], partner)

    def map_copy(m):
        return remote(
            mapbuf, maps.at[m], s_map.at[m], r_map.at[m], ahead if m == 0 else ahead2
        )

    def flag_copy(r):
        return remote(fbuf.at[r], fin.at[r], s_flag.at[r], r_flag.at[r], flip(1 << r))

    def group_copy(m):
        return remote(
            fbuf.at[ROUNDS],
            gin.at[m - 1],
            s_group.at[m - 1],
            r_group.at[m - 1],
            flip(m << ROUNDS),
        )

    def finish_round(r):
        flag_copy(r).wait_recv()
        fbuf[r + 1] = jnp.maximum(fbuf[r], fin[r])

    for m in range(len(offsets)):
        col_copy(m).start()

    def start_raw(u, carry):
        raw_copy(u).start()
        return carry

    lax.fori_loop(0, AHEAD, start_raw, 0)
    part_copy().start()

    def convert(ref, first, pos, count):
        h, l = split(ref[pl.ds(pos, count)])
        hi[pl.ds(first + pos, count)] = h
        lo[pl.ds(first + pos, count)] = l

    def convert_all(ref, first):
        def step(u, carry):
            convert(ref, first, u * CH, CH)
            return carry

        lax.fori_loop(0, STEPS, step, 0)

    hi[NONE] = jnp.zeros((BS, BS), jnp.bfloat16)
    lo[NONE] = jnp.zeros((BS, BS), jnp.bfloat16)

    for m in range(len(offsets)):
        col_copy(m).wait_recv()
    sub = lax.broadcasted_iota(i32, (8, 128), 0)
    lane = lax.broadcasted_iota(i32, (8, 128), 1)
    lane_col = lane + (RB * d - 64)

    def spread(tile, value):
        where = jnp.zeros((8, 128), f32)
        what = jnp.zeros((8, 128), i32)
        for t in range(NNZ):
            hit = jnp.broadcast_to(tile[:, t : t + 1], (8, 128)) == lane_col
            where = jnp.where(hit, 1.0, where)
            if value is not None:
                what = jnp.where(hit, value + t, what)
        return where, what

    next1, _ = spread(wcols[NEAR + s], None)
    next2, _ = spread(wcols[NEAR + 2 * s], None)

    def needed(readers, back):
        need = jnp.zeros((8, 128), f32)
        for j in range(RB):
            here = lane == 64 - RB * back * s + j
            row = jnp.zeros((1, 128), f32)
            for reader in readers:
                reads = jnp.max(jnp.where(here, reader, 0.0), axis=1, keepdims=True)
                row = jnp.maximum(row, jnp.max(reader * reads, axis=0, keepdims=True))
            need = jnp.where(sub == j, jnp.broadcast_to(row, (8, 128)), need)
        return need

    has_1, src_1 = spread(wcols[NEAR - s], sub * NNZ)
    has_2, src_2 = spread(wcols[NEAR - 2 * s], sub * NNZ + OWN)
    chosen = jnp.concatenate(
        [has_1 * needed([next1, next2], 1), has_2 * needed([next1], 2)], axis=0
    )
    square_row = lax.broadcasted_iota(i32, (128, 128), 0)
    square_lane = lax.broadcasted_iota(i32, (128, 128), 1)
    before = jnp.where(square_row < square_lane, 1.0, 0.0).astype(jnp.bfloat16)
    rank = jnp.dot(chosen.astype(jnp.bfloat16), before, preferred_element_type=f32)
    totals = jnp.sum(chosen, axis=1, keepdims=True)
    sub16 = lax.broadcasted_iota(i32, (16, 128), 0)
    count_1 = jnp.zeros((1, 1), f32)
    for j in range(RB):
        count_1 = count_1 + totals[j : j + 1, :]
    start_2 = jnp.maximum(count_1, float(X))
    for r in range(RB):
        rank = rank + jnp.where(
            jnp.logical_and(sub16 > r, sub16 < 8),
            jnp.broadcast_to(totals[r : r + 1, :], (16, 128)),
            0.0,
        )
        rank = rank + jnp.where(
            jnp.logical_and(sub16 >= 8, s * (sub16 - 8 - r) < 0),
            jnp.broadcast_to(totals[8 + r : 9 + r, :], (16, 128)),
            0.0,
        )
    rank = rank + jnp.where(sub16 >= 8, jnp.broadcast_to(start_2, (16, 128)), 0.0)
    taken = jnp.logical_and(chosen > 0.5, rank < CAP - 0.5)
    slot = jnp.where(taken, rank, -1.0)
    slot_int = slot.astype(i32)
    mapbuf[...] = slot_int
    for m in range(2):
        map_copy(m).start()
    order = p * (RB - 1 - (sub16 - 8)) + (1 - p) * (sub16 - 8)
    limit = jnp.where(
        sub16 >= 8, ESTEPS * PCH + PCH * jnp.maximum(order - 1, 0), OWN
    ).astype(f32)
    beyond = jnp.where(jnp.logical_and(chosen > 0.5, rank > limit - 0.5), 1.0, 0.0)
    over = jnp.max(jnp.max(beyond, axis=1, keepdims=True), axis=0, keepdims=True)
    fbuf[0] = jnp.broadcast_to(over, (8, 128))

    for tile in range(-(-CAP // 8)):
        found = jnp.zeros((8, 128), i32)
        for r in range(RB):
            hit = jnp.broadcast_to(slot_int[r : r + 1, :], (8, 128)) == sub + 8 * tile
            found = jnp.where(hit, jnp.broadcast_to(src_1[r : r + 1, :], (8, 128)), found)
            if tile * 8 >= X:
                hit = jnp.broadcast_to(slot_int[8 + r : 9 + r, :], (8, 128)) == sub + 8 * tile
                found = jnp.where(hit, jnp.broadcast_to(src_2[r : r + 1, :], (8, 128)), found)
        source = jnp.sum(found.astype(f32), axis=1, keepdims=True).astype(i32)
        inv_v[tile * 8 : tile * 8 + 8, :] = jnp.broadcast_to(source, (8, 128))
    to_inv = pltpu.make_async_copy(inv_v, inv, s_local.at[1])
    to_inv.start()
    to_inv.wait()

    part_copy().wait_recv()

    def pack_first(u, carry):
        for b in range(PCH):
            pool_out[u * PCH + b] = part[jnp.clip(inv[u * PCH + b, 0], 0, OWN - 1)]
        return carry

    lax.fori_loop(0, X // PCH, pack_first, 0)
    load.wait()
    convert_all(own, 0)
    convert_all(part, PART0)

    def lane_base(o):
        back = jnp.where(o >= 2, s, jnp.where(o <= -3, -2 * s, 0))
        return RB * (d + back) - 64

    def resolve(m, carry):
        i = m // NNZ
        r = jnp.clip(cols[i, lax.rem(m, NNZ)] - base, 0, SLOTS * RB - 1)
        w = lax.shift_right_logical(r, 2)
        row = w * 8 + lax.bitwise_and(r, 3)
        first = lane_base(s * (w - NEAR))
        for b in range(NNZ):
            found = tab[row, jnp.clip(cols[i, b] - first, 0, 127)]
            idx[m * NNZ + b] = jnp.clip(found, 0, NONE)
        return carry

    def take_raw_b(u):
        raw_fwd(u).wait_recv()
        convert(raw_b, RAW_B0, u * CH, CH)

    def build_table():
        for m in range(2):
            map_copy(m).wait_recv()

        def put(o, tile):
            at_row = pl.multiple_of((NEAR + s * o) * 8, 8)
            tab_v[pl.ds(at_row, 8), :] = jnp.where(sub < RB, jnp.clip(tile, 0, NONE), NONE)

        for o, first in ((0, 0), (-1, PART0), (1, RAW_A0), (-2, RAW_B0)):
            has, where = spread(wcols[NEAR + s * o], sub * NNZ + first)
            put(o, jnp.where(has > 0.5, where, NONE))
        for o, m, half, first in ((2, 0, 0, POOL_A0), (3, 0, 8, POOL_A0), (-3, 1, 0, POOL_B0)):
            got = maps[m, half : half + 8, :]
            put(o, jnp.where(got >= 0, got + first, NONE))
        to_tab = pltpu.make_async_copy(tab_v, tab, s_local.at[1])
        to_tab.start()
        to_tab.wait()

    for u in range(STEPS):
        raw_copy(u).wait_recv()
        raw_fwd(u).start()
        if u % 2 == 0:
            if u > 0:
                finish_round(u // 2 - 1)
            flag_copy(u // 2).start()
        if u + AHEAD < STEPS:
            raw_copy(u + AHEAD).start()
        else:
            pool_copy(u + AHEAD - STEPS).start()
        convert(raw_a, RAW_A0, u * CH, CH)
        if u > 0:
            take_raw_b(u - 1)
        if u == 3:
            build_table()
    take_raw_b(STEPS - 1)

    def pack_rest(u, carry):
        for b in range(PCH):
            source = inv[u * PCH + b, 0]
            pool_out[u * PCH + b] = jnp.where(
                source < OWN,
                part[jnp.clip(source, 0, OWN - 1)],
                raw_b[jnp.clip(source - OWN, 0, OWN - 1)],
            )
        pool_copy(u).start()
        return carry

    def take_pool_b(u):
        pool_fwd(u).wait_recv()
        convert(pool_b, POOL_B0, u * PCH, PCH)

    def tile(ref, index, count_a):
        return jnp.concatenate(
            [
                jnp.concatenate([ref[index[a][b]] for b in range(QB)], axis=1)
                for a in range(count_a)
            ],
            axis=0,
        )

    def block_at(i, a, b):
        return jnp.clip(idx[(i * NNZ + a) * NNZ + b], 0, NONE)

    def part_of(q):
        return pl.ds(q * QB * BS, QB * BS)

    def near_square(i, carry):
        keep = []
        for a in range(NNZ):
            r = jnp.clip(cols[i, a] - base, 0, SLOTS * RB - 1)
            o = s * (lax.shift_right_logical(r, 2) - NEAR)
            keep.append(jnp.logical_and(o > -3, o < 2))
        lhs_hi = jnp.concatenate([hi[i * NNZ + a] for a in range(NNZ)], axis=1)
        lhs_lo = jnp.concatenate([lo[i * NNZ + a] for a in range(NNZ)], axis=1)
        for q in range(NNZ // QB):
            index = [
                [
                    jnp.where(keep[a], block_at(i, a, q * QB + b), NONE)
                    for b in range(QB)
                ]
                for a in range(NNZ)
            ]
            sq[i, :, part_of(q)] = dot3(
                lhs_hi, lhs_lo, tile(hi, index, NNZ), tile(lo, index, NNZ)
            )
        return carry

    def add_rows(i, o, picks):
        coef = [
            jnp.clip(tab[NEAR * 8 + i, 64 + RB * o * s + j], 0, NONE) for j in picks
        ]
        lhs_hi = jnp.concatenate([hi[c] for c in coef], axis=1)
        lhs_lo = jnp.concatenate([lo[c] for c in coef], axis=1)
        first = lane_base(o)
        lanes = [jnp.clip(cols[i, b] - first, 0, 127) for b in range(NNZ)]
        for q in range(NNZ // QB):
            index = [
                [
                    jnp.clip(tab[(NEAR + o * s) * 8 + j, lanes[q * QB + b]], 0, NONE)
                    for b in range(QB)
                ]
                for j in picks
            ]
            sq[i, :, part_of(q)] += dot3(
                lhs_hi, lhs_lo, tile(hi, index, len(picks)), tile(lo, index, len(picks))
            )

    def pool_step(u, carry):
        pool_copy(u).wait_recv()
        pool_fwd(u).start()

        @pl.when(u + AHEAD < X // PCH)
        def _():
            pool_copy(u + AHEAD).start()

        @pl.when(u + AHEAD >= X // PCH)
        def _():
            pack_rest(u + AHEAD, 0)

        convert(pool_a, POOL_A0, u * PCH, PCH)

        @pl.when(u > 0)
        def _():
            take_pool_b(u - 1)

        lax.fori_loop(u * RB, (u + 1) * RB, resolve, 0)
        return carry

    finish_round(STEPS // 2 - 1)

    def pool_part(i, carry):
        lax.fori_loop(i * ASTEPS // RB, (i + 1) * ASTEPS // RB, pool_step, 0)
        near_square(i, 0)
        return carry

    lax.fori_loop(0, RB - 1, pool_part, 0)
    lax.fori_loop((RB - 1) * ASTEPS // RB, ASTEPS, pool_step, 0)
    for m in range(1, GROUPS):
        group_copy(m).start()
    lax.fori_loop(ASTEPS + AHEAD, PSTEPS, pack_rest, 0)
    near_square(RB - 1, 0)
    take_pool_b(ASTEPS - 1)

    def pool_square(i, carry):
        add_rows(i, 2, range(RB))
        add_rows(i, -3, range(RB))
        return carry

    lax.fori_loop(0, RB, pool_square, 0)


    def last_pool(u, carry):
        pool_copy(u).wait_recv()
        convert(pool_a, POOL_A0, u * PCH, PCH)
        return carry

    lax.fori_loop(ASTEPS, ESTEPS, last_pool, 0)

    def out_copy(i):
        rows = pl.ds(i * NNZ, NNZ)
        return pltpu.make_async_copy(own.at[rows], out_ref.at[rows], s_local.at[2 + i])

    def turn(t):
        return t * p + (RB - 1 - t) * (1 - p)

    def finish_row(t, count):
        i = turn(t)
        add_rows(i, 3, [turn(u) for u in range(count)])
        h, l = split(sq[i])
        sq_hi[...] = h
        sq_lo[...] = l
        for q in range(NNZ // QB):
            index = [
                [block_at(i, a, q * QB + b) for b in range(QB)]
                for a in range(NNZ)
            ]
            third = dot3(sq_hi[...], sq_lo[...], tile(hi, index, NNZ), tile(lo, index, NNZ))
            res = 3.0 * sq[i, :, part_of(q)] - 2.0 * third
            for b in range(QB):
                own[i * NNZ + q * QB + b] = res[:, b * BS : (b + 1) * BS]
        out_copy(i).start()

    finish_row(0, 1)
    finish_row(1, 2)
    lax.fori_loop(ESTEPS, ESTEPS + 1, last_pool, 0)
    finish_row(2, 3)
    lax.fori_loop(ESTEPS + 1, PSTEPS, last_pool, 0)
    finish_row(3, 4)
    over_all = fbuf[ROUNDS]
    for m in range(1, GROUPS):
        group_copy(m).wait_recv()
        over_all = jnp.maximum(over_all, gin[m - 1])
    flag_ref[0, 0] = jnp.max(over_all).astype(i32)

    def done_raw(u, carry):
        raw_copy(u).wait_send()
        raw_fwd(u).wait_send()
        return carry

    def done_pool(u, carry):
        pool_copy(u).wait_send()
        return carry

    def done_fwd(u, carry):
        pool_fwd(u).wait_send()
        return carry

    lax.fori_loop(0, STEPS, done_raw, 0)
    lax.fori_loop(0, PSTEPS, done_pool, 0)
    lax.fori_loop(0, ASTEPS, done_fwd, 0)
    part_copy().wait_send()
    for m in range(len(offsets)):
        col_copy(m).wait_send()
    for m in range(2):
        map_copy(m).wait_send()
    for r in range(ROUNDS):
        flag_copy(r).wait_send()
    for m in range(1, GROUPS):
        group_copy(m).wait_send()
    for i in range(RB):
        out_copy(i).wait()


def call_full(blocks, block_cols, n):
    dma = pltpu.SemaphoreType.DMA
    return pl.pallas_call(
        functools.partial(full_kernel, n),
        out_shape=jax.ShapeDtypeStruct((OWN, BS, BS), jnp.float32),
        in_specs=[
            pl.BlockSpec(memory_space=pl.ANY),
            pl.BlockSpec(memory_space=pltpu.VMEM),
            pl.BlockSpec(memory_space=pltpu.SMEM),
        ],
        out_specs=pl.BlockSpec(memory_space=pl.ANY),
        scratch_shapes=[
            pltpu.VMEM((SLOTS, OWN, BS, BS), jnp.float32),
            pltpu.VMEM((ZERO + 1, BS, BS), jnp.bfloat16),
            pltpu.VMEM((ZERO + 1, BS, BS), jnp.bfloat16),
            pltpu.VMEM((RB, BS, NNZ * BS), jnp.float32),
            pltpu.VMEM((BS, NNZ * BS), jnp.bfloat16),
            pltpu.VMEM((BS, NNZ * BS), jnp.bfloat16),
            pltpu.VMEM((8, 128), jnp.int32),
            pltpu.VMEM((SLOTS, 8, 128), jnp.int32),
            pltpu.VMEM((RB * TROWS + 8, 128), jnp.int32),
            pltpu.SMEM((RB * TROWS + 8, 128), jnp.int32),
            dma((6,)),
            dma((6,)),
            dma((2, STEPS)),
            dma((2, STEPS)),
            dma((3, STEPS)),
            dma((3, STEPS)),
            dma((1,)),
            dma((1,)),
            dma((2 + RB,)),
        ],
        compiler_params=pltpu.CompilerParams(
            collective_id=1, has_side_effects=True, vmem_limit_bytes=58 << 20
        ),
        name="mcweeny_full",
    )(blocks, block_cols, block_cols)


def call_fast(blocks, block_cols, n):
    dma = pltpu.SemaphoreType.DMA
    buffer = lambda count: pltpu.VMEM((count, BS, BS), jnp.float32)
    half = pltpu.VMEM((NONE + 1, BS, BS), jnp.bfloat16)
    rows = -(-CAP // 8) * 8
    return pl.pallas_call(
        functools.partial(fast_kernel, n),
        out_shape=[
            jax.ShapeDtypeStruct((OWN, BS, BS), jnp.float32),
            jax.ShapeDtypeStruct((1, 1), jnp.int32),
        ],
        in_specs=[
            pl.BlockSpec(memory_space=pl.ANY),
            pl.BlockSpec(memory_space=pltpu.VMEM),
            pl.BlockSpec(memory_space=pltpu.SMEM),
        ],
        out_specs=[
            pl.BlockSpec(memory_space=pl.ANY),
            pl.BlockSpec(memory_space=pltpu.SMEM),
        ],
        scratch_shapes=[
            buffer(OWN),
            buffer(OWN),
            buffer(OWN),
            buffer(OWN),
            buffer(CAP),
            buffer(OWN),
            buffer(CAP),
            half,
            half,
            pltpu.VMEM((RB, BS, NNZ * BS), jnp.float32),
            pltpu.VMEM((BS, NNZ * BS), jnp.bfloat16),
            pltpu.VMEM((BS, NNZ * BS), jnp.bfloat16),
            pltpu.VMEM((8, 128), jnp.int32),
            pltpu.VMEM((SLOTS, 8, 128), jnp.int32),
            pltpu.VMEM((16, 128), jnp.int32),
            pltpu.VMEM((2, 16, 128), jnp.int32),
            pltpu.VMEM((rows, 128), jnp.int32),
            pltpu.SMEM((rows, 128), jnp.int32),
            pltpu.VMEM((TROWS, 128), jnp.int32),
            pltpu.SMEM((TROWS, 128), jnp.int32),
            pltpu.SMEM((OWN * NNZ,), jnp.int32),
            pltpu.VMEM((ROUNDS + 1, 8, 128), jnp.float32),
            pltpu.VMEM((ROUNDS, 8, 128), jnp.float32),
            pltpu.VMEM((GROUPS - 1, 8, 128), jnp.float32),
            dma((6,)),
            dma((6,)),
            dma((2,)),
            dma((2,)),
            dma((STEPS,)),
            dma((STEPS,)),
            dma((PSTEPS,)),
            dma((PSTEPS,)),
            dma((STEPS,)),
            dma((STEPS,)),
            dma((ASTEPS,)),
            dma((ASTEPS,)),
            dma((1,)),
            dma((1,)),
            dma((ROUNDS,)),
            dma((ROUNDS,)),
            dma((GROUPS - 1,)),
            dma((GROUPS - 1,)),
            dma((2 + RB,)),
        ],
        compiler_params=pltpu.CompilerParams(
            collective_id=0, has_side_effects=True, vmem_limit_bytes=58 << 20
        ),
        name="mcweeny_fast",
    )(blocks, block_cols, block_cols)


def keep_kernel(src, dst, buf, got, put):
    parts = range(KEEP)
    rows = [pl.ds(i * (OWN // KEEP), OWN // KEEP) for i in parts]
    loads = [pltpu.make_async_copy(src.at[rows[i]], buf.at[rows[i]], got.at[i]) for i in parts]
    stores = [pltpu.make_async_copy(buf.at[rows[i]], dst.at[rows[i]], put.at[i]) for i in parts]
    for load in loads:
        load.start()
    for load, store in zip(loads, stores):
        load.wait()
        store.start()
    for store in stores:
        store.wait()


def keep(blocks):
    dma = pltpu.SemaphoreType.DMA
    return pl.pallas_call(
        keep_kernel,
        out_shape=jax.ShapeDtypeStruct(blocks.shape, blocks.dtype),
        in_specs=[pl.BlockSpec(memory_space=pl.ANY)],
        out_specs=pl.BlockSpec(memory_space=pl.ANY),
        scratch_shapes=[
            pltpu.VMEM((OWN, BS, BS), jnp.float32),
            dma((KEEP,)),
            dma((KEEP,)),
        ],
        compiler_params=pltpu.CompilerParams(vmem_limit_bytes=58 << 20),
        name="keep",
    )(blocks)


def body(density_blocks, block_cols, n):
    blocks = density_blocks.reshape(OWN, BS, BS)
    out, over = call_fast(blocks, block_cols, n)
    out = lax.cond(
        over[0, 0] > 0,
        lambda b, c, o: call_full(b, c, n),
        lambda b, c, o: o,
        blocks,
        block_cols,
        out,
    )
    return keep(out).reshape(RB, NNZ, BS, BS)


def solution(mesh):
    placed = (P("grid", None, None, None), P("grid", None))
    return jax.shard_map(
        functools.partial(body, n=mesh.shape["grid"]),
        mesh=mesh,
        in_specs=placed,
        out_specs=P("grid", None, None, None),
        check_vma=False,
    )
```

```python
import functools

import jax
import jax.numpy as jnp
from jax import lax
from jax.experimental import pallas as pl
from jax.experimental.pallas import tpu as pltpu
from jax.sharding import PartitionSpec as P

MESH = pl.DeviceIdType.MESH
BS = 128
NNZ = 12
NEAR = 3
RB = 4
OWN = RB * NNZ
SLOTS = 2 * NEAR + 1
ZERO = SLOTS * OWN
STEPS = 8
CH = OWN // STEPS
QB = 4
TROWS = SLOTS * 8


def split(x):
    high = x.astype(jnp.bfloat16)
    return high, (x - high.astype(jnp.float32)).astype(jnp.bfloat16)


def dot3(lhs_hi, lhs_lo, rhs_hi, rhs_lo):
    dot = functools.partial(jnp.dot, preferred_element_type=jnp.float32)
    return dot(lhs_hi, rhs_hi) + dot(lhs_lo, rhs_hi) + dot(lhs_hi, rhs_lo)


def full_kernel(
    n,
    x_ref,
    colv_ref,
    cols,
    out_ref,
    win,
    hi,
    lo,
    sq,
    sq_hi,
    sq_lo,
    colbuf,
    wcols,
    tab_v,
    tab,
    s_cols,
    r_cols,
    s_own,
    r_own,
    s_fwd,
    r_fwd,
    s_part,
    r_part,
    s_local,
):
    d = lax.axis_index("grid")
    p = lax.rem(d, 2)
    right, left = lax.rem(d + 2, n), lax.rem(d + n - 2, n)
    partner = d + 1 - 2 * p
    far_dev = lax.rem(d + n - 1 + 2 * p, n)
    far = 6 * p
    base = RB * (d - NEAR)
    offsets = (-3, -2, -1, 1, 2, 3)

    barrier = pltpu.get_barrier_semaphore()
    for off in offsets:
        pl.semaphore_signal(
            barrier, inc=1, device_id=(lax.rem(d + n + off, n),), device_id_type=MESH
        )
    load = pltpu.make_async_copy(x_ref, win.at[NEAR], s_local.at[0])
    load.start()
    colbuf[...] = jnp.full((8, 128), -1, jnp.int32)
    colbuf[0:RB, 0:NNZ] = colv_ref[...]
    wcols[NEAR] = colbuf[...]
    pl.semaphore_wait(barrier, len(offsets))

    def remote(src, dst, send, recv, dev):
        return pltpu.make_async_remote_copy(
            src_ref=src,
            dst_ref=dst,
            send_sem=send,
            recv_sem=recv,
            device_id=(dev,),
            device_id_type=MESH,
        )

    def col_copy(m):
        off = offsets[m]
        return remote(
            colbuf,
            wcols.at[NEAR - off],
            s_cols.at[m],
            r_cols.at[m],
            lax.rem(d + n + off, n),
        )

    for m in range(len(offsets)):
        col_copy(m).start()

    def at_right(u):
        return (RB - 1 - u // 2) * NNZ + lax.rem(u, 2) * CH

    def at_left(u):
        return (u // 2) * NNZ + lax.rem(u, 2) * CH

    def own_right(u):
        pos = at_right(u)
        return remote(
            x_ref.at[pl.ds(pos, CH)],
            win.at[1, pl.ds(pos, CH)],
            s_own.at[0, u],
            r_own.at[0, u],
            right,
        )

    def own_left(u):
        pos = at_left(u)
        return remote(
            x_ref.at[pl.ds(pos, CH)],
            win.at[5, pl.ds(pos, CH)],
            s_own.at[1, u],
            r_own.at[1, u],
            left,
        )

    def part_copy():
        return remote(
            x_ref, win.at[2 + 2 * p], s_part.at[0], r_part.at[0], partner
        )

    def start_own(u, carry):
        own_right(u).start()
        own_left(u).start()
        return carry

    lax.fori_loop(0, STEPS, start_own, 0)
    part_copy().start()

    def convert(slot, pos, count):
        h, l = split(win[slot, pl.ds(pos, count)])
        hi[pl.ds(slot * OWN + pos, count)] = h
        lo[pl.ds(slot * OWN + pos, count)] = l

    def convert_all(slot):
        def step(u, carry):
            convert(slot, u * CH, CH)
            return carry

        lax.fori_loop(0, STEPS, step, 0)

    hi[ZERO] = jnp.zeros((BS, BS), jnp.bfloat16)
    lo[ZERO] = jnp.zeros((BS, BS), jnp.bfloat16)
    load.wait()
    convert_all(NEAR)

    for m in range(len(offsets)):
        col_copy(m).wait()
    row_in_tile = lax.broadcasted_iota(jnp.int32, (8, 128), 0)
    own_tile = wcols[NEAR]
    for i in range(RB):
        own_cols = jnp.broadcast_to(own_tile[i : i + 1, :], (8, 128))

        def slot_table(s, carry):
            tile = wcols[s]
            found = jnp.full((8, 128), ZERO, jnp.int32)
            first = (s * RB + row_in_tile) * NNZ
            for t in range(NNZ):
                col = jnp.broadcast_to(tile[:, t : t + 1], (8, 128))
                found = jnp.where(col == own_cols, first + t, found)
            tab_v[pl.ds(pl.multiple_of(i * TROWS + s * 8, 8), 8), :] = jnp.where(
                row_in_tile < RB, found, ZERO
            )
            return carry

        lax.fori_loop(0, SLOTS, slot_table, 0)
    lane = lax.broadcasted_iota(jnp.int32, (8, 128), 1)
    coef = jnp.full((8, 128), ZERO, jnp.int32)
    for a in range(NNZ):
        col = jnp.broadcast_to(own_tile[:, a : a + 1], (8, 128))
        coef = jnp.where(col == lane + base, NEAR * OWN + row_in_tile * NNZ + a, coef)
    tab_v[RB * TROWS : RB * TROWS + 8, :] = jnp.where(row_in_tile < RB, coef, ZERO)
    to_smem = pltpu.make_async_copy(tab_v, tab, s_local.at[1])
    to_smem.start()
    to_smem.wait()

    def fwd_from_left(u):
        pos = at_right(u)
        return remote(
            win.at[1, pl.ds(pos, CH)],
            win.at[2 * p, pl.ds(pos, CH)],
            s_fwd.at[0, u],
            r_fwd.at[0, u],
            partner,
        )

    def fwd_from_right(u):
        pos = at_left(u)
        return remote(
            win.at[5, pl.ds(pos, CH)],
            win.at[4 + 2 * p, pl.ds(pos, CH)],
            s_fwd.at[1, u],
            r_fwd.at[1, u],
            partner,
        )

    def fwd_far(u):
        pos = at_right(u) * p + at_left(u) * (1 - p)
        return remote(
            win.at[5 - 4 * p, pl.ds(pos, CH)],
            win.at[6 - 6 * p, pl.ds(pos, CH)],
            s_fwd.at[2, u],
            r_fwd.at[2, u],
            far_dev,
        )

    def take_partner(u):
        fwd_from_left(u).wait_recv()
        convert(2 - 2 * p, at_right(u), CH)
        fwd_from_right(u).wait_recv()
        convert(6 - 2 * p, at_left(u), CH)

    part_copy().wait_recv()
    convert_all(4 - 2 * p)

    def near_step(u, carry):
        own_right(u).wait_recv()
        own_left(u).wait_recv()
        fwd_from_left(u).start()
        fwd_from_right(u).start()
        fwd_far(u).start()
        convert(1, at_right(u), CH)
        convert(5, at_left(u), CH)
        take_partner(u)
        return carry

    lax.fori_loop(0, STEPS, near_step, 0)

    def tile(ref, index, count_a):
        return jnp.concatenate(
            [
                jnp.concatenate([ref[index[a][b]] for b in range(QB)], axis=1)
                for a in range(count_a)
            ],
            axis=0,
        )

    def window_rows(i):
        rows = []
        for a in range(NNZ):
            r = jnp.clip(cols[i, a] - base, 0, SLOTS * RB - 1)
            rows.append((r, i * TROWS + r + lax.shift_left(lax.shift_right_logical(r, 2), 2)))
        return rows

    def part(q):
        return pl.ds(pl.multiple_of(q * QB * BS, QB * BS), QB * BS)

    def near_square(i, carry):
        rows = window_rows(i)

        def columns(q, carry):
            index = []
            for r, row in rows:
                in_far = jnp.logical_and(r >= far * RB, r < far * RB + RB)
                index.append(
                    [jnp.where(in_far, ZERO, tab[row, q * QB + b]) for b in range(QB)]
                )
            own = NEAR * OWN + i * NNZ
            lhs_hi = jnp.concatenate([hi[own + a] for a in range(NNZ)], axis=1)
            lhs_lo = jnp.concatenate([lo[own + a] for a in range(NNZ)], axis=1)
            sq[i, :, part(q)] = dot3(
                lhs_hi, lhs_lo, tile(hi, index, NNZ), tile(lo, index, NNZ)
            )
            return carry

        lax.fori_loop(0, NNZ // QB, columns, 0)
        return carry

    lax.fori_loop(0, RB, near_square, 0)

    def far_square(i, j):
        at = tab[RB * TROWS + i, far * RB + j]
        lhs_hi, lhs_lo = hi[at], lo[at]

        def columns(q, carry):
            index = [[tab[i * TROWS + far * 8 + j, q * QB + b] for b in range(QB)]]
            sq[i, :, part(q)] += dot3(lhs_hi, lhs_lo, tile(hi, index, 1), tile(lo, index, 1))
            return carry

        lax.fori_loop(0, NNZ // QB, columns, 0)

    def out_copy(i):
        rows = pl.ds(i * NNZ, NNZ)
        return pltpu.make_async_copy(win.at[NEAR, rows], out_ref.at[rows], s_local.at[2 + i])

    def cube(i):
        h, l = split(sq[i])
        sq_hi[...] = h
        sq_lo[...] = l
        rows = window_rows(i)

        def columns(q, carry):
            index = [[tab[row, q * QB + b] for b in range(QB)] for _, row in rows]
            third = dot3(sq_hi[...], sq_lo[...], tile(hi, index, NNZ), tile(lo, index, NNZ))
            res = 3.0 * sq[i, :, part(q)] - 2.0 * third
            for b in range(QB):
                win[NEAR, i * NNZ + q * QB + b] = res[:, b * BS : (b + 1) * BS]
            return carry

        lax.fori_loop(0, NNZ // QB, columns, 0)
        out_copy(i).start()

    def far_step(t, carry):
        j = (RB - 1 - t) * (1 - p) + t * p
        for half in range(2):
            u = 2 * t + half
            pos = at_right(u) * (1 - p) + at_left(u) * p
            fwd_far(u).wait_recv()
            convert(far, pos, CH)

        def row(m, carry):
            far_square(m * (1 - p) + (RB - 1 - m) * p, j)
            return carry

        lax.fori_loop(0, RB - t, row, 0)
        last = RB - 1 - t
        cube(last * (1 - p) + (RB - 1 - last) * p)
        return carry

    lax.fori_loop(0, RB, far_step, 0)

    def finish(u, carry):
        own_right(u).wait_send()
        own_left(u).wait_send()
        fwd_from_left(u).wait_send()
        fwd_from_right(u).wait_send()
        fwd_far(u).wait_send()
        return carry

    lax.fori_loop(0, STEPS, finish, 0)
    part_copy().wait_send()
    for i in range(RB):
        out_copy(i).wait()


X = 24
CAP = 68
PCH = 4
PSTEPS = CAP // PCH
ASTEPS = OWN // PCH
ESTEPS = (OWN + NNZ) // PCH
PART0, RAW_A0, RAW_B0, POOL_A0, POOL_B0 = 48, 96, 144, 192, 192 + CAP
NONE = POOL_B0 + OWN
AHEAD = 4
ROUNDS = 4
GROUPS = 8
KEEP = 8
PAD = -100000


def fast_kernel(
    n,
    x_ref,
    colv_ref,
    cols,
    out_ref,
    flag_ref,
    own,
    part,
    raw_a,
    raw_b,
    pool_a,
    pool_b,
    pool_out,
    hi,
    lo,
    sq,
    sq_hi,
    sq_lo,
    colbuf,
    wcols,
    mapbuf,
    maps,
    inv_v,
    inv,
    tab_v,
    tab,
    idx,
    fbuf,
    fin,
    gin,
    s_cols,
    r_cols,
    s_map,
    r_map,
    s_raw,
    r_raw,
    s_pool,
    r_pool,
    s_fraw,
    r_fraw,
    s_fpool,
    r_fpool,
    s_part,
    r_part,
    s_flag,
    r_flag,
    s_group,
    r_group,
    s_local,
):
    f32, i32 = jnp.float32, jnp.int32
    d = lax.axis_index("grid")
    p = lax.rem(d, 2)
    s = 2 * p - 1
    base = RB * (d - NEAR)
    offsets = (-3, -2, -1, 1, 2, 3)

    def at(off):
        return lax.rem(d + n + off, n)

    def flip(change):
        to = d
        for r in range(7):
            if (change >> r) % 2:
                to = to + (1 << r) - (2 << r) * lax.rem(d // (1 << r), 2)
        return to

    ahead, ahead2, partner = at(s), at(2 * s), at(-s)

    barrier = pltpu.get_barrier_semaphore()
    greeted = [at(off) for off in offsets] + [flip(1 << r) for r in range(2, ROUNDS)]
    greeted = greeted + [flip(m << ROUNDS) for m in range(1, GROUPS)]
    for dev in greeted:
        pl.semaphore_signal(barrier, inc=1, device_id=(dev,), device_id_type=MESH)
    load = pltpu.make_async_copy(x_ref, own, s_local.at[0])
    load.start()
    colbuf[...] = jnp.full((8, 128), PAD, i32)
    colbuf[0:RB, 0:NNZ] = colv_ref[...]
    wcols[NEAR] = colbuf[...]
    pl.semaphore_wait(barrier, len(greeted))

    def remote(src, dst, send, recv, dev):
        return pltpu.make_async_remote_copy(
            src_ref=src,
            dst_ref=dst,
            send_sem=send,
            recv_sem=recv,
            device_id=(dev,),
            device_id_type=MESH,
        )

    def col_copy(m):
        off = offsets[m]
        return remote(colbuf, wcols.at[NEAR - off], s_cols.at[m], r_cols.at[m], at(off))

    def part_copy():
        return remote(x_ref, part, s_part.at[0], r_part.at[0], partner)

    def raw_copy(u):
        rows = pl.ds(u * CH, CH)
        return remote(x_ref.at[rows], raw_a.at[rows], s_raw.at[u], r_raw.at[u], ahead)

    def raw_fwd(u):
        rows = pl.ds(u * CH, CH)
        return remote(raw_a.at[rows], raw_b.at[rows], s_fraw.at[u], r_fraw.at[u], partner)

    def pool_copy(u):
        rows = pl.ds(u * PCH, PCH)
        return remote(pool_out.at[rows], pool_a.at[rows], s_pool.at[u], r_pool.at[u], ahead)

    def pool_fwd(u):
        rows = pl.ds(u * PCH, PCH)
        return remote(pool_a.at[rows], pool_b.at[rows], s_fpool.at[u], r_fpool.at[u], partner)

    def map_copy(m):
        return remote(
            mapbuf, maps.at[m], s_map.at[m], r_map.at[m], ahead if m == 0 else ahead2
        )

    def flag_copy(r):
        return remote(fbuf.at[r], fin.at[r], s_flag.at[r], r_flag.at[r], flip(1 << r))

    def group_copy(m):
        return remote(
            fbuf.at[ROUNDS],
            gin.at[m - 1],
            s_group.at[m - 1],
            r_group.at[m - 1],
            flip(m << ROUNDS),
        )

    def finish_round(r):
        flag_copy(r).wait_recv()
        fbuf[r + 1] = jnp.maximum(fbuf[r], fin[r])

    for m in range(len(offsets)):
        col_copy(m).start()

    def start_raw(u, carry):
        raw_copy(u).start()
        return carry

    lax.fori_loop(0, AHEAD, start_raw, 0)
    part_copy().start()

    def convert(ref, first, pos, count):
        h, l = split(ref[pl.ds(pos, count)])
        hi[pl.ds(first + pos, count)] = h
        lo[pl.ds(first + pos, count)] = l

    def convert_all(ref, first):
        def step(u, carry):
            convert(ref, first, u * CH, CH)
            return carry

        lax.fori_loop(0, STEPS, step, 0)

    hi[NONE] = jnp.zeros((BS, BS), jnp.bfloat16)
    lo[NONE] = jnp.zeros((BS, BS), jnp.bfloat16)

    for m in range(len(offsets)):
        col_copy(m).wait_recv()
    sub = lax.broadcasted_iota(i32, (8, 128), 0)
    lane = lax.broadcasted_iota(i32, (8, 128), 1)
    lane_col = lane + (RB * d - 64)

    def spread(tile, value):
        where = jnp.zeros((8, 128), f32)
        what = jnp.zeros((8, 128), i32)
        for t in range(NNZ):
            hit = jnp.broadcast_to(tile[:, t : t + 1], (8, 128)) == lane_col
            where = jnp.where(hit, 1.0, where)
            if value is not None:
                what = jnp.where(hit, value + t, what)
        return where, what

    next1, _ = spread(wcols[NEAR + s], None)
    next2, _ = spread(wcols[NEAR + 2 * s], None)

    def needed(readers, back):
        need = jnp.zeros((8, 128), f32)
        for j in range(RB):
            here = lane == 64 - RB * back * s + j
            row = jnp.zeros((1, 128), f32)
            for reader in readers:
                reads = jnp.max(jnp.where(here, reader, 0.0), axis=1, keepdims=True)
                row = jnp.maximum(row, jnp.max(reader * reads, axis=0, keepdims=True))
            need = jnp.where(sub == j, jnp.broadcast_to(row, (8, 128)), need)
        return need

    has_1, src_1 = spread(wcols[NEAR - s], sub * NNZ)
    has_2, src_2 = spread(wcols[NEAR - 2 * s], sub * NNZ + OWN)
    chosen = jnp.concatenate(
        [has_1 * needed([next1, next2], 1), has_2 * needed([next1], 2)], axis=0
    )
    square_row = lax.broadcasted_iota(i32, (128, 128), 0)
    square_lane = lax.broadcasted_iota(i32, (128, 128), 1)
    before = jnp.where(square_row < square_lane, 1.0, 0.0).astype(jnp.bfloat16)
    rank = jnp.dot(chosen.astype(jnp.bfloat16), before, preferred_element_type=f32)
    totals = jnp.sum(chosen, axis=1, keepdims=True)
    sub16 = lax.broadcasted_iota(i32, (16, 128), 0)
    count_1 = jnp.zeros((1, 1), f32)
    for j in range(RB):
        count_1 = count_1 + totals[j : j + 1, :]
    start_2 = jnp.maximum(count_1, float(X))
    for r in range(RB):
        rank = rank + jnp.where(
            jnp.logical_and(sub16 > r, sub16 < 8),
            jnp.broadcast_to(totals[r : r + 1, :], (16, 128)),
            0.0,
        )
        rank = rank + jnp.where(
            jnp.logical_and(sub16 >= 8, s * (sub16 - 8 - r) < 0),
            jnp.broadcast_to(totals[8 + r : 9 + r, :], (16, 128)),
            0.0,
        )
    rank = rank + jnp.where(sub16 >= 8, jnp.broadcast_to(start_2, (16, 128)), 0.0)
    taken = jnp.logical_and(chosen > 0.5, rank < CAP - 0.5)
    slot = jnp.where(taken, rank, -1.0)
    slot_int = slot.astype(i32)
    mapbuf[...] = slot_int
    for m in range(2):
        map_copy(m).start()
    order = p * (RB - 1 - (sub16 - 8)) + (1 - p) * (sub16 - 8)
    limit = jnp.where(
        sub16 >= 8, ESTEPS * PCH + PCH * jnp.maximum(order - 1, 0), OWN
    ).astype(f32)
    beyond = jnp.where(jnp.logical_and(chosen > 0.5, rank > limit - 0.5), 1.0, 0.0)
    over = jnp.max(jnp.max(beyond, axis=1, keepdims=True), axis=0, keepdims=True)
    fbuf[0] = jnp.broadcast_to(over, (8, 128))

    for tile in range(-(-CAP // 8)):
        found = jnp.zeros((8, 128), i32)
        for r in range(RB):
            hit = jnp.broadcast_to(slot_int[r : r + 1, :], (8, 128)) == sub + 8 * tile
            found = jnp.where(hit, jnp.broadcast_to(src_1[r : r + 1, :], (8, 128)), found)
            if tile * 8 >= X:
                hit = jnp.broadcast_to(slot_int[8 + r : 9 + r, :], (8, 128)) == sub + 8 * tile
                found = jnp.where(hit, jnp.broadcast_to(src_2[r : r + 1, :], (8, 128)), found)
        source = jnp.sum(found.astype(f32), axis=1, keepdims=True).astype(i32)
        inv_v[tile * 8 : tile * 8 + 8, :] = jnp.broadcast_to(source, (8, 128))
    to_inv = pltpu.make_async_copy(inv_v, inv, s_local.at[1])
    to_inv.start()
    to_inv.wait()

    part_copy().wait_recv()

    def pack_first(u, carry):
        for b in range(PCH):
            pool_out[u * PCH + b] = part[jnp.clip(inv[u * PCH + b, 0], 0, OWN - 1)]
        return carry

    lax.fori_loop(0, X // PCH, pack_first, 0)
    load.wait()
    convert_all(own, 0)
    convert_all(part, PART0)

    def lane_base(o):
        back = jnp.where(o >= 2, s, jnp.where(o <= -3, -2 * s, 0))
        return RB * (d + back) - 64

    def resolve(m, carry):
        i = m // NNZ
        r = jnp.clip(cols[i, lax.rem(m, NNZ)] - base, 0, SLOTS * RB - 1)
        w = lax.shift_right_logical(r, 2)
        row = w * 8 + lax.bitwise_and(r, 3)
        first = lane_base(s * (w - NEAR))
        for b in range(NNZ):
            found = tab[row, jnp.clip(cols[i, b] - first, 0, 127)]
            idx[m * NNZ + b] = jnp.clip(found, 0, NONE)
        return carry

    def take_raw_b(u):
        raw_fwd(u).wait_recv()
        convert(raw_b, RAW_B0, u * CH, CH)

    def build_table():
        for m in range(2):
            map_copy(m).wait_recv()

        def put(o, tile):
            at_row = pl.multiple_of((NEAR + s * o) * 8, 8)
            tab_v[pl.ds(at_row, 8), :] = jnp.where(sub < RB, jnp.clip(tile, 0, NONE), NONE)

        for o, first in ((0, 0), (-1, PART0), (1, RAW_A0), (-2, RAW_B0)):
            has, where = spread(wcols[NEAR + s * o], sub * NNZ + first)
            put(o, jnp.where(has > 0.5, where, NONE))
        for o, m, half, first in ((2, 0, 0, POOL_A0), (3, 0, 8, POOL_A0), (-3, 1, 0, POOL_B0)):
            got = maps[m, half : half + 8, :]
            put(o, jnp.where(got >= 0, got + first, NONE))
        to_tab = pltpu.make_async_copy(tab_v, tab, s_local.at[1])
        to_tab.start()
        to_tab.wait()

    for u in range(STEPS):
        raw_copy(u).wait_recv()
        raw_fwd(u).start()
        if u % 2 == 0:
            if u > 0:
                finish_round(u // 2 - 1)
            flag_copy(u // 2).start()
        if u + AHEAD < STEPS:
            raw_copy(u + AHEAD).start()
        else:
            pool_copy(u + AHEAD - STEPS).start()
        convert(raw_a, RAW_A0, u * CH, CH)
        if u > 0:
            take_raw_b(u - 1)
        if u == 3:
            build_table()
    take_raw_b(STEPS - 1)

    def pack_rest(u, carry):
        for b in range(PCH):
            source = inv[u * PCH + b, 0]
            pool_out[u * PCH + b] = jnp.where(
                source < OWN,
                part[jnp.clip(source, 0, OWN - 1)],
                raw_b[jnp.clip(source - OWN, 0, OWN - 1)],
            )
        pool_copy(u).start()
        return carry

    def take_pool_b(u):
        pool_fwd(u).wait_recv()
        convert(pool_b, POOL_B0, u * PCH, PCH)

    def tile(ref, index, count_a):
        return jnp.concatenate(
            [
                jnp.concatenate([ref[index[a][b]] for b in range(QB)], axis=1)
                for a in range(count_a)
            ],
            axis=0,
        )

    def block_at(i, a, b):
        return jnp.clip(idx[(i * NNZ + a) * NNZ + b], 0, NONE)

    def part_of(q):
        return pl.ds(q * QB * BS, QB * BS)

    def near_square(i, carry):
        keep = []
        for a in range(NNZ):
            r = jnp.clip(cols[i, a] - base, 0, SLOTS * RB - 1)
            o = s * (lax.shift_right_logical(r, 2) - NEAR)
            keep.append(jnp.logical_and(o > -3, o < 2))
        lhs_hi = jnp.concatenate([hi[i * NNZ + a] for a in range(NNZ)], axis=1)
        lhs_lo = jnp.concatenate([lo[i * NNZ + a] for a in range(NNZ)], axis=1)
        for q in range(NNZ // QB):
            index = [
                [
                    jnp.where(keep[a], block_at(i, a, q * QB + b), NONE)
                    for b in range(QB)
                ]
                for a in range(NNZ)
            ]
            sq[i, :, part_of(q)] = dot3(
                lhs_hi, lhs_lo, tile(hi, index, NNZ), tile(lo, index, NNZ)
            )
        return carry

    def add_rows(i, o, picks):
        coef = [
            jnp.clip(tab[NEAR * 8 + i, 64 + RB * o * s + j], 0, NONE) for j in picks
        ]
        lhs_hi = jnp.concatenate([hi[c] for c in coef], axis=1)
        lhs_lo = jnp.concatenate([lo[c] for c in coef], axis=1)
        first = lane_base(o)
        lanes = [jnp.clip(cols[i, b] - first, 0, 127) for b in range(NNZ)]
        for q in range(NNZ // QB):
            index = [
                [
                    jnp.clip(tab[(NEAR + o * s) * 8 + j, lanes[q * QB + b]], 0, NONE)
                    for b in range(QB)
                ]
                for j in picks
            ]
            sq[i, :, part_of(q)] += dot3(
                lhs_hi, lhs_lo, tile(hi, index, len(picks)), tile(lo, index, len(picks))
            )

    def pool_step(u, carry):
        pool_copy(u).wait_recv()
        pool_fwd(u).start()

        @pl.when(u + AHEAD < X // PCH)
        def _():
            pool_copy(u + AHEAD).start()

        @pl.when(u + AHEAD >= X // PCH)
        def _():
            pack_rest(u + AHEAD, 0)

        convert(pool_a, POOL_A0, u * PCH, PCH)

        @pl.when(u > 0)
        def _():
            take_pool_b(u - 1)

        lax.fori_loop(u * RB, (u + 1) * RB, resolve, 0)
        return carry

    finish_round(STEPS // 2 - 1)

    def pool_part(i, carry):
        lax.fori_loop(i * ASTEPS // RB, (i + 1) * ASTEPS // RB, pool_step, 0)
        near_square(i, 0)
        return carry

    lax.fori_loop(0, RB - 1, pool_part, 0)
    lax.fori_loop((RB - 1) * ASTEPS // RB, ASTEPS, pool_step, 0)
    for m in range(1, GROUPS):
        group_copy(m).start()
    lax.fori_loop(ASTEPS + AHEAD, PSTEPS, pack_rest, 0)
    near_square(RB - 1, 0)
    take_pool_b(ASTEPS - 1)

    def pool_square(i, carry):
        add_rows(i, 2, range(RB))
        add_rows(i, -3, range(RB))
        return carry

    lax.fori_loop(0, RB, pool_square, 0)


    def last_pool(u, carry):
        pool_copy(u).wait_recv()
        convert(pool_a, POOL_A0, u * PCH, PCH)
        return carry

    lax.fori_loop(ASTEPS, ESTEPS, last_pool, 0)

    def out_copy(i):
        rows = pl.ds(i * NNZ, NNZ)
        return pltpu.make_async_copy(own.at[rows], out_ref.at[rows], s_local.at[2 + i])

    def turn(t):
        return t * p + (RB - 1 - t) * (1 - p)

    def finish_row(t, count):
        i = turn(t)
        add_rows(i, 3, [turn(u) for u in range(count)])
        h, l = split(sq[i])
        sq_hi[...] = h
        sq_lo[...] = l
        for q in range(NNZ // QB):
            index = [
                [block_at(i, a, q * QB + b) for b in range(QB)]
                for a in range(NNZ)
            ]
            third = dot3(sq_hi[...], sq_lo[...], tile(hi, index, NNZ), tile(lo, index, NNZ))
            res = 3.0 * sq[i, :, part_of(q)] - 2.0 * third
            for b in range(QB):
                own[i * NNZ + q * QB + b] = res[:, b * BS : (b + 1) * BS]
        out_copy(i).start()

    finish_row(0, 1)
    finish_row(1, 2)
    lax.fori_loop(ESTEPS, ESTEPS + 1, last_pool, 0)
    finish_row(2, 3)
    lax.fori_loop(ESTEPS + 1, PSTEPS, last_pool, 0)
    finish_row(3, 4)
    over_all = fbuf[ROUNDS]
    for m in range(1, GROUPS):
        group_copy(m).wait_recv()
        over_all = jnp.maximum(over_all, gin[m - 1])
    flag_ref[0, 0] = jnp.max(over_all).astype(i32)

    def done_raw(u, carry):
        raw_copy(u).wait_send()
        raw_fwd(u).wait_send()
        return carry

    def done_pool(u, carry):
        pool_copy(u).wait_send()
        return carry

    def done_fwd(u, carry):
        pool_fwd(u).wait_send()
        return carry

    lax.fori_loop(0, STEPS, done_raw, 0)
    lax.fori_loop(0, PSTEPS, done_pool, 0)
    lax.fori_loop(0, ASTEPS, done_fwd, 0)
    part_copy().wait_send()
    for m in range(len(offsets)):
        col_copy(m).wait_send()
    for m in range(2):
        map_copy(m).wait_send()
    for r in range(ROUNDS):
        flag_copy(r).wait_send()
    for m in range(1, GROUPS):
        group_copy(m).wait_send()
    for i in range(RB):
        out_copy(i).wait()


def call_full(blocks, block_cols, n):
    dma = pltpu.SemaphoreType.DMA
    return pl.pallas_call(
        functools.partial(full_kernel, n),
        out_shape=jax.ShapeDtypeStruct((OWN, BS, BS), jnp.float32),
        in_specs=[
            pl.BlockSpec(memory_space=pl.ANY),
            pl.BlockSpec(memory_space=pltpu.VMEM),
            pl.BlockSpec(memory_space=pltpu.SMEM),
        ],
        out_specs=pl.BlockSpec(memory_space=pl.ANY),
        scratch_shapes=[
            pltpu.VMEM((SLOTS, OWN, BS, BS), jnp.float32),
            pltpu.VMEM((ZERO + 1, BS, BS), jnp.bfloat16),
            pltpu.VMEM((ZERO + 1, BS, BS), jnp.bfloat16),
            pltpu.VMEM((RB, BS, NNZ * BS), jnp.float32),
            pltpu.VMEM((BS, NNZ * BS), jnp.bfloat16),
            pltpu.VMEM((BS, NNZ * BS), jnp.bfloat16),
            pltpu.VMEM((8, 128), jnp.int32),
            pltpu.VMEM((SLOTS, 8, 128), jnp.int32),
            pltpu.VMEM((RB * TROWS + 8, 128), jnp.int32),
            pltpu.SMEM((RB * TROWS + 8, 128), jnp.int32),
            dma((6,)),
            dma((6,)),
            dma((2, STEPS)),
            dma((2, STEPS)),
            dma((3, STEPS)),
            dma((3, STEPS)),
            dma((1,)),
            dma((1,)),
            dma((2 + RB,)),
        ],
        compiler_params=pltpu.CompilerParams(
            collective_id=1, has_side_effects=True, vmem_limit_bytes=58 << 20
        ),
        name="mcweeny_full",
    )(blocks, block_cols, block_cols)


def call_fast(blocks, block_cols, n):
    dma = pltpu.SemaphoreType.DMA
    buffer = lambda count: pltpu.VMEM((count, BS, BS), jnp.float32)
    half = pltpu.VMEM((NONE + 1, BS, BS), jnp.bfloat16)
    rows = -(-CAP // 8) * 8
    return pl.pallas_call(
        functools.partial(fast_kernel, n),
        out_shape=[
            jax.ShapeDtypeStruct((OWN, BS, BS), jnp.float32),
            jax.ShapeDtypeStruct((1, 1), jnp.int32),
        ],
        in_specs=[
            pl.BlockSpec(memory_space=pl.ANY),
            pl.BlockSpec(memory_space=pltpu.VMEM),
            pl.BlockSpec(memory_space=pltpu.SMEM),
        ],
        out_specs=[
            pl.BlockSpec(memory_space=pl.ANY),
            pl.BlockSpec(memory_space=pltpu.SMEM),
        ],
        scratch_shapes=[
            buffer(OWN),
            buffer(OWN),
            buffer(OWN),
            buffer(OWN),
            buffer(CAP),
            buffer(OWN),
            buffer(CAP),
            half,
            half,
            pltpu.VMEM((RB, BS, NNZ * BS), jnp.float32),
            pltpu.VMEM((BS, NNZ * BS), jnp.bfloat16),
            pltpu.VMEM((BS, NNZ * BS), jnp.bfloat16),
            pltpu.VMEM((8, 128), jnp.int32),
            pltpu.VMEM((SLOTS, 8, 128), jnp.int32),
            pltpu.VMEM((16, 128), jnp.int32),
            pltpu.VMEM((2, 16, 128), jnp.int32),
            pltpu.VMEM((rows, 128), jnp.int32),
            pltpu.SMEM((rows, 128), jnp.int32),
            pltpu.VMEM((TROWS, 128), jnp.int32),
            pltpu.SMEM((TROWS, 128), jnp.int32),
            pltpu.SMEM((OWN * NNZ,), jnp.int32),
            pltpu.VMEM((ROUNDS + 1, 8, 128), jnp.float32),
            pltpu.VMEM((ROUNDS, 8, 128), jnp.float32),
            pltpu.VMEM((GROUPS - 1, 8, 128), jnp.float32),
            dma((6,)),
            dma((6,)),
            dma((2,)),
            dma((2,)),
            dma((STEPS,)),
            dma((STEPS,)),
            dma((PSTEPS,)),
            dma((PSTEPS,)),
            dma((STEPS,)),
            dma((STEPS,)),
            dma((ASTEPS,)),
            dma((ASTEPS,)),
            dma((1,)),
            dma((1,)),
            dma((ROUNDS,)),
            dma((ROUNDS,)),
            dma((GROUPS - 1,)),
            dma((GROUPS - 1,)),
            dma((2 + RB,)),
        ],
        compiler_params=pltpu.CompilerParams(
            collective_id=0, has_side_effects=True, vmem_limit_bytes=58 << 20
        ),
        name="mcweeny_fast",
    )(blocks, block_cols, block_cols)


def keep_kernel(src, dst, buf, got, put):
    parts = range(KEEP)
    rows = [pl.ds(i * (OWN // KEEP), OWN // KEEP) for i in parts]
    loads = [pltpu.make_async_copy(src.at[rows[i]], buf.at[rows[i]], got.at[i]) for i in parts]
    stores = [pltpu.make_async_copy(buf.at[rows[i]], dst.at[rows[i]], put.at[i]) for i in parts]
    for load in loads:
        load.start()
    for load, store in zip(loads, stores):
        load.wait()
        store.start()
    for store in stores:
        store.wait()


def keep(blocks):
    dma = pltpu.SemaphoreType.DMA
    return pl.pallas_call(
        keep_kernel,
        out_shape=jax.ShapeDtypeStruct(blocks.shape, blocks.dtype),
        in_specs=[pl.BlockSpec(memory_space=pl.ANY)],
        out_specs=pl.BlockSpec(memory_space=pl.ANY),
        scratch_shapes=[
            pltpu.VMEM((OWN, BS, BS), jnp.float32),
            dma((KEEP,)),
            dma((KEEP,)),
        ],
        compiler_params=pltpu.CompilerParams(vmem_limit_bytes=58 << 20),
        name="keep",
    )(blocks)


def body(density_blocks, block_cols, n):
    blocks = density_blocks.reshape(OWN, BS, BS)
    out, over = call_fast(blocks, block_cols, n)
    out = lax.cond(
        over[0, 0] > 0,
        lambda b, c, o: call_full(b, c, n),
        lambda b, c, o: o,
        blocks,
        block_cols,
        out,
    )
    return keep(out).reshape(RB, NNZ, BS, BS)


def solution(mesh):
    placed = (P("grid", None, None, None), P("grid", None))
    return jax.shard_map(
        functools.partial(body, n=mesh.shape["grid"]),
        mesh=mesh,
        in_specs=placed,
        out_specs=P("grid", None, None, None),
        check_vma=False,
    )
```

```python
import functools

import jax
import jax.numpy as jnp
from jax import lax
from jax.experimental import pallas as pl
from jax.experimental.pallas import tpu as pltpu
from jax.sharding import PartitionSpec as P

MESH = pl.DeviceIdType.MESH
BS = 128
NNZ = 12
NEAR = 3
RB = 4
OWN = RB * NNZ
SLOTS = 2 * NEAR + 1
ZERO = SLOTS * OWN
STEPS = 8
CH = OWN // STEPS
QB = 4
TROWS = SLOTS * 8


def split(x):
    high = x.astype(jnp.bfloat16)
    return high, (x - high.astype(jnp.float32)).astype(jnp.bfloat16)


def dot3(lhs_hi, lhs_lo, rhs_hi, rhs_lo):
    dot = functools.partial(jnp.dot, preferred_element_type=jnp.float32)
    return dot(lhs_hi, rhs_hi) + dot(lhs_lo, rhs_hi) + dot(lhs_hi, rhs_lo)


def full_kernel(
    n,
    x_ref,
    colv_ref,
    cols,
    out_ref,
    win,
    hi,
    lo,
    sq,
    sq_hi,
    sq_lo,
    colbuf,
    wcols,
    tab_v,
    tab,
    s_cols,
    r_cols,
    s_own,
    r_own,
    s_fwd,
    r_fwd,
    s_part,
    r_part,
    s_local,
):
    d = lax.axis_index("grid")
    p = lax.rem(d, 2)
    right, left = lax.rem(d + 2, n), lax.rem(d + n - 2, n)
    partner = d + 1 - 2 * p
    far_dev = lax.rem(d + n - 1 + 2 * p, n)
    far = 6 * p
    base = RB * (d - NEAR)
    offsets = (-3, -2, -1, 1, 2, 3)

    barrier = pltpu.get_barrier_semaphore()
    for off in offsets:
        pl.semaphore_signal(
            barrier, inc=1, device_id=(lax.rem(d + n + off, n),), device_id_type=MESH
        )
    load = pltpu.make_async_copy(x_ref, win.at[NEAR], s_local.at[0])
    load.start()
    colbuf[...] = jnp.full((8, 128), -1, jnp.int32)
    colbuf[0:RB, 0:NNZ] = colv_ref[...]
    wcols[NEAR] = colbuf[...]
    pl.semaphore_wait(barrier, len(offsets))

    def remote(src, dst, send, recv, dev):
        return pltpu.make_async_remote_copy(
            src_ref=src,
            dst_ref=dst,
            send_sem=send,
            recv_sem=recv,
            device_id=(dev,),
            device_id_type=MESH,
        )

    def col_copy(m):
        off = offsets[m]
        return remote(
            colbuf,
            wcols.at[NEAR - off],
            s_cols.at[m],
            r_cols.at[m],
            lax.rem(d + n + off, n),
        )

    for m in range(len(offsets)):
        col_copy(m).start()

    def at_right(u):
        return (RB - 1 - u // 2) * NNZ + lax.rem(u, 2) * CH

    def at_left(u):
        return (u // 2) * NNZ + lax.rem(u, 2) * CH

    def own_right(u):
        pos = at_right(u)
        return remote(
            x_ref.at[pl.ds(pos, CH)],
            win.at[1, pl.ds(pos, CH)],
            s_own.at[0, u],
            r_own.at[0, u],
            right,
        )

    def own_left(u):
        pos = at_left(u)
        return remote(
            x_ref.at[pl.ds(pos, CH)],
            win.at[5, pl.ds(pos, CH)],
            s_own.at[1, u],
            r_own.at[1, u],
            left,
        )

    def part_copy():
        return remote(
            x_ref, win.at[2 + 2 * p], s_part.at[0], r_part.at[0], partner
        )

    def start_own(u, carry):
        own_right(u).start()
        own_left(u).start()
        return carry

    lax.fori_loop(0, STEPS, start_own, 0)
    part_copy().start()

    def convert(slot, pos, count):
        h, l = split(win[slot, pl.ds(pos, count)])
        hi[pl.ds(slot * OWN + pos, count)] = h
        lo[pl.ds(slot * OWN + pos, count)] = l

    def convert_all(slot):
        def step(u, carry):
            convert(slot, u * CH, CH)
            return carry

        lax.fori_loop(0, STEPS, step, 0)

    hi[ZERO] = jnp.zeros((BS, BS), jnp.bfloat16)
    lo[ZERO] = jnp.zeros((BS, BS), jnp.bfloat16)
    load.wait()
    convert_all(NEAR)

    for m in range(len(offsets)):
        col_copy(m).wait()
    row_in_tile = lax.broadcasted_iota(jnp.int32, (8, 128), 0)
    own_tile = wcols[NEAR]
    for i in range(RB):
        own_cols = jnp.broadcast_to(own_tile[i : i + 1, :], (8, 128))

        def slot_table(s, carry):
            tile = wcols[s]
            found = jnp.full((8, 128), ZERO, jnp.int32)
            first = (s * RB + row_in_tile) * NNZ
            for t in range(NNZ):
                col = jnp.broadcast_to(tile[:, t : t + 1], (8, 128))
                found = jnp.where(col == own_cols, first + t, found)
            tab_v[pl.ds(pl.multiple_of(i * TROWS + s * 8, 8), 8), :] = jnp.where(
                row_in_tile < RB, found, ZERO
            )
            return carry

        lax.fori_loop(0, SLOTS, slot_table, 0)
    lane = lax.broadcasted_iota(jnp.int32, (8, 128), 1)
    coef = jnp.full((8, 128), ZERO, jnp.int32)
    for a in range(NNZ):
        col = jnp.broadcast_to(own_tile[:, a : a + 1], (8, 128))
        coef = jnp.where(col == lane + base, NEAR * OWN + row_in_tile * NNZ + a, coef)
    tab_v[RB * TROWS : RB * TROWS + 8, :] = jnp.where(row_in_tile < RB, coef, ZERO)
    to_smem = pltpu.make_async_copy(tab_v, tab, s_local.at[1])
    to_smem.start()
    to_smem.wait()

    def fwd_from_left(u):
        pos = at_right(u)
        return remote(
            win.at[1, pl.ds(pos, CH)],
            win.at[2 * p, pl.ds(pos, CH)],
            s_fwd.at[0, u],
            r_fwd.at[0, u],
            partner,
        )

    def fwd_from_right(u):
        pos = at_left(u)
        return remote(
            win.at[5, pl.ds(pos, CH)],
            win.at[4 + 2 * p, pl.ds(pos, CH)],
            s_fwd.at[1, u],
            r_fwd.at[1, u],
            partner,
        )

    def fwd_far(u):
        pos = at_right(u) * p + at_left(u) * (1 - p)
        return remote(
            win.at[5 - 4 * p, pl.ds(pos, CH)],
            win.at[6 - 6 * p, pl.ds(pos, CH)],
            s_fwd.at[2, u],
            r_fwd.at[2, u],
            far_dev,
        )

    def take_partner(u):
        fwd_from_left(u).wait_recv()
        convert(2 - 2 * p, at_right(u), CH)
        fwd_from_right(u).wait_recv()
        convert(6 - 2 * p, at_left(u), CH)

    part_copy().wait_recv()
    convert_all(4 - 2 * p)

    def near_step(u, carry):
        own_right(u).wait_recv()
        own_left(u).wait_recv()
        fwd_from_left(u).start()
        fwd_from_right(u).start()
        fwd_far(u).start()
        convert(1, at_right(u), CH)
        convert(5, at_left(u), CH)
        take_partner(u)
        return carry

    lax.fori_loop(0, STEPS, near_step, 0)

    def tile(ref, index, count_a):
        return jnp.concatenate(
            [
                jnp.concatenate([ref[index[a][b]] for b in range(QB)], axis=1)
                for a in range(count_a)
            ],
            axis=0,
        )

    def window_rows(i):
        rows = []
        for a in range(NNZ):
            r = jnp.clip(cols[i, a] - base, 0, SLOTS * RB - 1)
            rows.append((r, i * TROWS + r + lax.shift_left(lax.shift_right_logical(r, 2), 2)))
        return rows

    def part(q):
        return pl.ds(pl.multiple_of(q * QB * BS, QB * BS), QB * BS)

    def near_square(i, carry):
        rows = window_rows(i)

        def columns(q, carry):
            index = []
            for r, row in rows:
                in_far = jnp.logical_and(r >= far * RB, r < far * RB + RB)
                index.append(
                    [jnp.where(in_far, ZERO, tab[row, q * QB + b]) for b in range(QB)]
                )
            own = NEAR * OWN + i * NNZ
            lhs_hi = jnp.concatenate([hi[own + a] for a in range(NNZ)], axis=1)
            lhs_lo = jnp.concatenate([lo[own + a] for a in range(NNZ)], axis=1)
            sq[i, :, part(q)] = dot3(
                lhs_hi, lhs_lo, tile(hi, index, NNZ), tile(lo, index, NNZ)
            )
            return carry

        lax.fori_loop(0, NNZ // QB, columns, 0)
        return carry

    lax.fori_loop(0, RB, near_square, 0)

    def far_square(i, j):
        at = tab[RB * TROWS + i, far * RB + j]
        lhs_hi, lhs_lo = hi[at], lo[at]

        def columns(q, carry):
            index = [[tab[i * TROWS + far * 8 + j, q * QB + b] for b in range(QB)]]
            sq[i, :, part(q)] += dot3(lhs_hi, lhs_lo, tile(hi, index, 1), tile(lo, index, 1))
            return carry

        lax.fori_loop(0, NNZ // QB, columns, 0)

    def out_copy(i):
        rows = pl.ds(i * NNZ, NNZ)
        return pltpu.make_async_copy(win.at[NEAR, rows], out_ref.at[rows], s_local.at[2 + i])

    def cube(i):
        h, l = split(sq[i])
        sq_hi[...] = h
        sq_lo[...] = l
        rows = window_rows(i)

        def columns(q, carry):
            index = [[tab[row, q * QB + b] for b in range(QB)] for _, row in rows]
            third = dot3(sq_hi[...], sq_lo[...], tile(hi, index, NNZ), tile(lo, index, NNZ))
            res = 3.0 * sq[i, :, part(q)] - 2.0 * third
            for b in range(QB):
                win[NEAR, i * NNZ + q * QB + b] = res[:, b * BS : (b + 1) * BS]
            return carry

        lax.fori_loop(0, NNZ // QB, columns, 0)
        out_copy(i).start()

    def far_step(t, carry):
        j = (RB - 1 - t) * (1 - p) + t * p
        for half in range(2):
            u = 2 * t + half
            pos = at_right(u) * (1 - p) + at_left(u) * p
            fwd_far(u).wait_recv()
            convert(far, pos, CH)

        def row(m, carry):
            far_square(m * (1 - p) + (RB - 1 - m) * p, j)
            return carry

        lax.fori_loop(0, RB - t, row, 0)
        last = RB - 1 - t
        cube(last * (1 - p) + (RB - 1 - last) * p)
        return carry

    lax.fori_loop(0, RB, far_step, 0)

    def finish(u, carry):
        own_right(u).wait_send()
        own_left(u).wait_send()
        fwd_from_left(u).wait_send()
        fwd_from_right(u).wait_send()
        fwd_far(u).wait_send()
        return carry

    lax.fori_loop(0, STEPS, finish, 0)
    part_copy().wait_send()
    for i in range(RB):
        out_copy(i).wait()


X = 24
CAP = 68
PCH = 4
PSTEPS = CAP // PCH
ASTEPS = OWN // PCH
ESTEPS = (OWN + NNZ) // PCH
PART0, RAW_A0, RAW_B0, POOL_A0, POOL_B0 = 48, 96, 144, 192, 192 + CAP
NONE = POOL_B0 + OWN
AHEAD = 4
ROUNDS = 4
GROUPS = 8
KEEP = 8
PAD = -100000


def fast_kernel(
    n,
    x_ref,
    colv_ref,
    cols,
    out_ref,
    flag_ref,
    own,
    part,
    raw_a,
    raw_b,
    pool_a,
    pool_b,
    pool_out,
    hi,
    lo,
    sq,
    sq_hi,
    sq_lo,
    colbuf,
    wcols,
    mapbuf,
    maps,
    inv_v,
    inv,
    tab_v,
    tab,
    idx,
    fbuf,
    fin,
    gin,
    s_cols,
    r_cols,
    s_map,
    r_map,
    s_raw,
    r_raw,
    s_pool,
    r_pool,
    s_fraw,
    r_fraw,
    s_fpool,
    r_fpool,
    s_part,
    r_part,
    s_flag,
    r_flag,
    s_group,
    r_group,
    s_local,
):
    f32, i32 = jnp.float32, jnp.int32
    d = lax.axis_index("grid")
    p = lax.rem(d, 2)
    s = 2 * p - 1
    base = RB * (d - NEAR)
    offsets = (-3, -2, -1, 1, 2, 3)

    def at(off):
        return lax.rem(d + n + off, n)

    def flip(change):
        to = d
        for r in range(7):
            if (change >> r) % 2:
                to = to + (1 << r) - (2 << r) * lax.rem(d // (1 << r), 2)
        return to

    ahead, ahead2, partner = at(s), at(2 * s), at(-s)

    barrier = pltpu.get_barrier_semaphore()
    greeted = [at(off) for off in offsets] + [flip(1 << r) for r in range(2, ROUNDS)]
    greeted = greeted + [flip(m << ROUNDS) for m in range(1, GROUPS)]
    for dev in greeted:
        pl.semaphore_signal(barrier, inc=1, device_id=(dev,), device_id_type=MESH)
    load = pltpu.make_async_copy(x_ref, own, s_local.at[0])
    load.start()
    colbuf[...] = jnp.full((8, 128), PAD, i32)
    colbuf[0:RB, 0:NNZ] = colv_ref[...]
    wcols[NEAR] = colbuf[...]
    pl.semaphore_wait(barrier, len(greeted))

    def remote(src, dst, send, recv, dev):
        return pltpu.make_async_remote_copy(
            src_ref=src,
            dst_ref=dst,
            send_sem=send,
            recv_sem=recv,
            device_id=(dev,),
            device_id_type=MESH,
        )

    def col_copy(m):
        off = offsets[m]
        return remote(colbuf, wcols.at[NEAR - off], s_cols.at[m], r_cols.at[m], at(off))

    def part_copy():
        return remote(x_ref, part, s_part.at[0], r_part.at[0], partner)

    def raw_copy(u):
        rows = pl.ds(u * CH, CH)
        return remote(x_ref.at[rows], raw_a.at[rows], s_raw.at[u], r_raw.at[u], ahead)

    def raw_fwd(u):
        rows = pl.ds(u * CH, CH)
        return remote(raw_a.at[rows], raw_b.at[rows], s_fraw.at[u], r_fraw.at[u], partner)

    def pool_copy(u):
        rows = pl.ds(u * PCH, PCH)
        return remote(pool_out.at[rows], pool_a.at[rows], s_pool.at[u], r_pool.at[u], ahead)

    def pool_fwd(u):
        rows = pl.ds(u * PCH, PCH)
        return remote(pool_a.at[rows], pool_b.at[rows], s_fpool.at[u], r_fpool.at[u], partner)

    def map_copy(m):
        return remote(
            mapbuf, maps.at[m], s_map.at[m], r_map.at[m], ahead if m == 0 else ahead2
        )

    def flag_copy(r):
        return remote(fbuf.at[r], fin.at[r], s_flag.at[r], r_flag.at[r], flip(1 << r))

    def group_copy(m):
        return remote(
            fbuf.at[ROUNDS],
            gin.at[m - 1],
            s_group.at[m - 1],
            r_group.at[m - 1],
            flip(m << ROUNDS),
        )

    def finish_round(r):
        flag_copy(r).wait_recv()
        fbuf[r + 1] = jnp.maximum(fbuf[r], fin[r])

    for m in range(len(offsets)):
        col_copy(m).start()

    def start_raw(u, carry):
        raw_copy(u).start()
        return carry

    lax.fori_loop(0, AHEAD, start_raw, 0)
    part_copy().start()

    def convert(ref, first, pos, count):
        h, l = split(ref[pl.ds(pos, count)])
        hi[pl.ds(first + pos, count)] = h
        lo[pl.ds(first + pos, count)] = l

    def convert_all(ref, first):
        def step(u, carry):
            convert(ref, first, u * CH, CH)
            return carry

        lax.fori_loop(0, STEPS, step, 0)

    hi[NONE] = jnp.zeros((BS, BS), jnp.bfloat16)
    lo[NONE] = jnp.zeros((BS, BS), jnp.bfloat16)

    for m in range(len(offsets)):
        col_copy(m).wait_recv()
    sub = lax.broadcasted_iota(i32, (8, 128), 0)
    lane = lax.broadcasted_iota(i32, (8, 128), 1)
    lane_col = lane + (RB * d - 64)

    def spread(tile, value):
        where = jnp.zeros((8, 128), f32)
        what = jnp.zeros((8, 128), i32)
        for t in range(NNZ):
            hit = jnp.broadcast_to(tile[:, t : t + 1], (8, 128)) == lane_col
            where = jnp.where(hit, 1.0, where)
            if value is not None:
                what = jnp.where(hit, value + t, what)
        return where, what

    next1, _ = spread(wcols[NEAR + s], None)
    next2, _ = spread(wcols[NEAR + 2 * s], None)

    def needed(readers, back):
        need = jnp.zeros((8, 128), f32)
        for j in range(RB):
            here = lane == 64 - RB * back * s + j
            row = jnp.zeros((1, 128), f32)
            for reader in readers:
                reads = jnp.max(jnp.where(here, reader, 0.0), axis=1, keepdims=True)
                row = jnp.maximum(row, jnp.max(reader * reads, axis=0, keepdims=True))
            need = jnp.where(sub == j, jnp.broadcast_to(row, (8, 128)), need)
        return need

    has_1, src_1 = spread(wcols[NEAR - s], sub * NNZ)
    has_2, src_2 = spread(wcols[NEAR - 2 * s], sub * NNZ + OWN)
    chosen = jnp.concatenate(
        [has_1 * needed([next1, next2], 1), has_2 * needed([next1], 2)], axis=0
    )
    square_row = lax.broadcasted_iota(i32, (128, 128), 0)
    square_lane = lax.broadcasted_iota(i32, (128, 128), 1)
    before = jnp.where(square_row < square_lane, 1.0, 0.0).astype(jnp.bfloat16)
    rank = jnp.dot(chosen.astype(jnp.bfloat16), before, preferred_element_type=f32)
    totals = jnp.sum(chosen, axis=1, keepdims=True)
    sub16 = lax.broadcasted_iota(i32, (16, 128), 0)
    count_1 = jnp.zeros((1, 1), f32)
    for j in range(RB):
        count_1 = count_1 + totals[j : j + 1, :]
    start_2 = jnp.maximum(count_1, float(X))
    for r in range(RB):
        rank = rank + jnp.where(
            jnp.logical_and(sub16 > r, sub16 < 8),
            jnp.broadcast_to(totals[r : r + 1, :], (16, 128)),
            0.0,
        )
        rank = rank + jnp.where(
            jnp.logical_and(sub16 >= 8, s * (sub16 - 8 - r) < 0),
            jnp.broadcast_to(totals[8 + r : 9 + r, :], (16, 128)),
            0.0,
        )
    rank = rank + jnp.where(sub16 >= 8, jnp.broadcast_to(start_2, (16, 128)), 0.0)
    taken = jnp.logical_and(chosen > 0.5, rank < CAP - 0.5)
    slot = jnp.where(taken, rank, -1.0)
    slot_int = slot.astype(i32)
    mapbuf[...] = slot_int
    for m in range(2):
        map_copy(m).start()
    order = p * (RB - 1 - (sub16 - 8)) + (1 - p) * (sub16 - 8)
    limit = jnp.where(
        sub16 >= 8, ESTEPS * PCH + PCH * jnp.maximum(order - 1, 0), OWN
    ).astype(f32)
    beyond = jnp.where(jnp.logical_and(chosen > 0.5, rank > limit - 0.5), 1.0, 0.0)
    over = jnp.max(jnp.max(beyond, axis=1, keepdims=True), axis=0, keepdims=True)
    fbuf[0] = jnp.broadcast_to(over, (8, 128))

    for tile in range(-(-CAP // 8)):
        found = jnp.zeros((8, 128), i32)
        for r in range(RB):
            hit = jnp.broadcast_to(slot_int[r : r + 1, :], (8, 128)) == sub + 8 * tile
            found = jnp.where(hit, jnp.broadcast_to(src_1[r : r + 1, :], (8, 128)), found)
            if tile * 8 >= X:
                hit = jnp.broadcast_to(slot_int[8 + r : 9 + r, :], (8, 128)) == sub + 8 * tile
                found = jnp.where(hit, jnp.broadcast_to(src_2[r : r + 1, :], (8, 128)), found)
        source = jnp.sum(found.astype(f32), axis=1, keepdims=True).astype(i32)
        inv_v[tile * 8 : tile * 8 + 8, :] = jnp.broadcast_to(source, (8, 128))
    to_inv = pltpu.make_async_copy(inv_v, inv, s_local.at[1])
    to_inv.start()
    to_inv.wait()

    part_copy().wait_recv()

    def pack_first(u, carry):
        for b in range(PCH):
            pool_out[u * PCH + b] = part[jnp.clip(inv[u * PCH + b, 0], 0, OWN - 1)]
        return carry

    lax.fori_loop(0, X // PCH, pack_first, 0)
    load.wait()
    convert_all(own, 0)
    convert_all(part, PART0)

    def lane_base(o):
        back = jnp.where(o >= 2, s, jnp.where(o <= -3, -2 * s, 0))
        return RB * (d + back) - 64

    def resolve(m, carry):
        i = m // NNZ
        r = jnp.clip(cols[i, lax.rem(m, NNZ)] - base, 0, SLOTS * RB - 1)
        w = lax.shift_right_logical(r, 2)
        row = w * 8 + lax.bitwise_and(r, 3)
        first = lane_base(s * (w - NEAR))
        for b in range(NNZ):
            found = tab[row, jnp.clip(cols[i, b] - first, 0, 127)]
            idx[m * NNZ + b] = jnp.clip(found, 0, NONE)
        return carry

    def take_raw_b(u):
        raw_fwd(u).wait_recv()
        convert(raw_b, RAW_B0, u * CH, CH)

    def build_table():
        for m in range(2):
            map_copy(m).wait_recv()

        def put(o, tile):
            at_row = pl.multiple_of((NEAR + s * o) * 8, 8)
            tab_v[pl.ds(at_row, 8), :] = jnp.where(sub < RB, jnp.clip(tile, 0, NONE), NONE)

        for o, first in ((0, 0), (-1, PART0), (1, RAW_A0), (-2, RAW_B0)):
            has, where = spread(wcols[NEAR + s * o], sub * NNZ + first)
            put(o, jnp.where(has > 0.5, where, NONE))
        for o, m, half, first in ((2, 0, 0, POOL_A0), (3, 0, 8, POOL_A0), (-3, 1, 0, POOL_B0)):
            got = maps[m, half : half + 8, :]
            put(o, jnp.where(got >= 0, got + first, NONE))
        to_tab = pltpu.make_async_copy(tab_v, tab, s_local.at[1])
        to_tab.start()
        to_tab.wait()

    for u in range(STEPS):
        raw_copy(u).wait_recv()
        raw_fwd(u).start()
        if u % 2 == 0:
            if u > 0:
                finish_round(u // 2 - 1)
            flag_copy(u // 2).start()
        if u + AHEAD < STEPS:
            raw_copy(u + AHEAD).start()
        else:
            pool_copy(u + AHEAD - STEPS).start()
        convert(raw_a, RAW_A0, u * CH, CH)
        if u > 0:
            take_raw_b(u - 1)
        if u == 3:
            build_table()
    take_raw_b(STEPS - 1)

    def pack_rest(u, carry):
        for b in range(PCH):
            source = inv[u * PCH + b, 0]
            pool_out[u * PCH + b] = jnp.where(
                source < OWN,
                part[jnp.clip(source, 0, OWN - 1)],
                raw_b[jnp.clip(source - OWN, 0, OWN - 1)],
            )
        pool_copy(u).start()
        return carry

    def take_pool_b(u):
        pool_fwd(u).wait_recv()
        convert(pool_b, POOL_B0, u * PCH, PCH)

    def tile(ref, index, count_a):
        return jnp.concatenate(
            [
                jnp.concatenate([ref[index[a][b]] for b in range(QB)], axis=1)
                for a in range(count_a)
            ],
            axis=0,
        )

    def block_at(i, a, b):
        return jnp.clip(idx[(i * NNZ + a) * NNZ + b], 0, NONE)

    def part_of(q):
        return pl.ds(q * QB * BS, QB * BS)

    def near_square(i, carry):
        keep = []
        for a in range(NNZ):
            r = jnp.clip(cols[i, a] - base, 0, SLOTS * RB - 1)
            o = s * (lax.shift_right_logical(r, 2) - NEAR)
            keep.append(jnp.logical_and(o > -3, o < 2))
        lhs_hi = jnp.concatenate([hi[i * NNZ + a] for a in range(NNZ)], axis=1)
        lhs_lo = jnp.concatenate([lo[i * NNZ + a] for a in range(NNZ)], axis=1)
        for q in range(NNZ // QB):
            index = [
                [
                    jnp.where(keep[a], block_at(i, a, q * QB + b), NONE)
                    for b in range(QB)
                ]
                for a in range(NNZ)
            ]
            sq[i, :, part_of(q)] = dot3(
                lhs_hi, lhs_lo, tile(hi, index, NNZ), tile(lo, index, NNZ)
            )
        return carry

    def add_rows(i, o, picks):
        coef = [
            jnp.clip(tab[NEAR * 8 + i, 64 + RB * o * s + j], 0, NONE) for j in picks
        ]
        lhs_hi = jnp.concatenate([hi[c] for c in coef], axis=1)
        lhs_lo = jnp.concatenate([lo[c] for c in coef], axis=1)
        first = lane_base(o)
        lanes = [jnp.clip(cols[i, b] - first, 0, 127) for b in range(NNZ)]
        for q in range(NNZ // QB):
            index = [
                [
                    jnp.clip(tab[(NEAR + o * s) * 8 + j, lanes[q * QB + b]], 0, NONE)
                    for b in range(QB)
                ]
                for j in picks
            ]
            sq[i, :, part_of(q)] += dot3(
                lhs_hi, lhs_lo, tile(hi, index, len(picks)), tile(lo, index, len(picks))
            )

    def pool_step(u, carry):
        pool_copy(u).wait_recv()
        pool_fwd(u).start()

        @pl.when(u + AHEAD < X // PCH)
        def _():
            pool_copy(u + AHEAD).start()

        @pl.when(u + AHEAD >= X // PCH)
        def _():
            pack_rest(u + AHEAD, 0)

        convert(pool_a, POOL_A0, u * PCH, PCH)

        @pl.when(u > 0)
        def _():
            take_pool_b(u - 1)

        lax.fori_loop(jnp.minimum(u * 6, OWN), jnp.minimum(u * 6 + 6, OWN), resolve, 0)
        return carry

    finish_round(STEPS // 2 - 1)

    def pool_part(i, carry):
        lax.fori_loop(2 * i, 2 * i + 2, pool_step, 0)
        near_square(i, 0)
        return carry

    lax.fori_loop(0, RB, pool_part, 0)
    lax.fori_loop(2 * RB, ASTEPS, pool_step, 0)
    for m in range(1, GROUPS):
        group_copy(m).start()
    lax.fori_loop(ASTEPS + AHEAD, PSTEPS, pack_rest, 0)

    def ahead_square(i, carry):
        add_rows(i, 2, range(RB))
        return carry

    def behind_square(i, carry):
        add_rows(i, -3, range(RB))
        return carry

    lax.fori_loop(0, RB, ahead_square, 0)
    take_pool_b(ASTEPS - 1)
    lax.fori_loop(0, RB, behind_square, 0)


    def last_pool(u, carry):
        pool_copy(u).wait_recv()
        convert(pool_a, POOL_A0, u * PCH, PCH)
        return carry

    lax.fori_loop(ASTEPS, ESTEPS, last_pool, 0)

    def out_copy(i):
        rows = pl.ds(i * NNZ, NNZ)
        return pltpu.make_async_copy(own.at[rows], out_ref.at[rows], s_local.at[2 + i])

    def turn(t):
        return t * p + (RB - 1 - t) * (1 - p)

    def finish_row(t, count):
        i = turn(t)
        add_rows(i, 3, [turn(u) for u in range(count)])
        h, l = split(sq[i])
        sq_hi[...] = h
        sq_lo[...] = l
        for q in range(NNZ // QB):
            index = [
                [block_at(i, a, q * QB + b) for b in range(QB)]
                for a in range(NNZ)
            ]
            third = dot3(sq_hi[...], sq_lo[...], tile(hi, index, NNZ), tile(lo, index, NNZ))
            res = 3.0 * sq[i, :, part_of(q)] - 2.0 * third
            for b in range(QB):
                own[i * NNZ + q * QB + b] = res[:, b * BS : (b + 1) * BS]
        out_copy(i).start()

    finish_row(0, 1)
    finish_row(1, 2)
    lax.fori_loop(ESTEPS, ESTEPS + 1, last_pool, 0)
    finish_row(2, 3)
    lax.fori_loop(ESTEPS + 1, PSTEPS, last_pool, 0)
    finish_row(3, 4)
    over_all = fbuf[ROUNDS]
    for m in range(1, GROUPS):
        group_copy(m).wait_recv()
        over_all = jnp.maximum(over_all, gin[m - 1])
    flag_ref[0, 0] = jnp.max(over_all).astype(i32)

    def done_raw(u, carry):
        raw_copy(u).wait_send()
        raw_fwd(u).wait_send()
        return carry

    def done_pool(u, carry):
        pool_copy(u).wait_send()
        return carry

    def done_fwd(u, carry):
        pool_fwd(u).wait_send()
        return carry

    lax.fori_loop(0, STEPS, done_raw, 0)
    lax.fori_loop(0, PSTEPS, done_pool, 0)
    lax.fori_loop(0, ASTEPS, done_fwd, 0)
    part_copy().wait_send()
    for m in range(len(offsets)):
        col_copy(m).wait_send()
    for m in range(2):
        map_copy(m).wait_send()
    for r in range(ROUNDS):
        flag_copy(r).wait_send()
    for m in range(1, GROUPS):
        group_copy(m).wait_send()
    for i in range(RB):
        out_copy(i).wait()


def call_full(blocks, block_cols, n):
    dma = pltpu.SemaphoreType.DMA
    return pl.pallas_call(
        functools.partial(full_kernel, n),
        out_shape=jax.ShapeDtypeStruct((OWN, BS, BS), jnp.float32),
        in_specs=[
            pl.BlockSpec(memory_space=pl.ANY),
            pl.BlockSpec(memory_space=pltpu.VMEM),
            pl.BlockSpec(memory_space=pltpu.SMEM),
        ],
        out_specs=pl.BlockSpec(memory_space=pl.ANY),
        scratch_shapes=[
            pltpu.VMEM((SLOTS, OWN, BS, BS), jnp.float32),
            pltpu.VMEM((ZERO + 1, BS, BS), jnp.bfloat16),
            pltpu.VMEM((ZERO + 1, BS, BS), jnp.bfloat16),
            pltpu.VMEM((RB, BS, NNZ * BS), jnp.float32),
            pltpu.VMEM((BS, NNZ * BS), jnp.bfloat16),
            pltpu.VMEM((BS, NNZ * BS), jnp.bfloat16),
            pltpu.VMEM((8, 128), jnp.int32),
            pltpu.VMEM((SLOTS, 8, 128), jnp.int32),
            pltpu.VMEM((RB * TROWS + 8, 128), jnp.int32),
            pltpu.SMEM((RB * TROWS + 8, 128), jnp.int32),
            dma((6,)),
            dma((6,)),
            dma((2, STEPS)),
            dma((2, STEPS)),
            dma((3, STEPS)),
            dma((3, STEPS)),
            dma((1,)),
            dma((1,)),
            dma((2 + RB,)),
        ],
        compiler_params=pltpu.CompilerParams(
            collective_id=1, has_side_effects=True, vmem_limit_bytes=58 << 20
        ),
        name="mcweeny_full",
    )(blocks, block_cols, block_cols)


def call_fast(blocks, block_cols, n):
    dma = pltpu.SemaphoreType.DMA
    buffer = lambda count: pltpu.VMEM((count, BS, BS), jnp.float32)
    half = pltpu.VMEM((NONE + 1, BS, BS), jnp.bfloat16)
    rows = -(-CAP // 8) * 8
    return pl.pallas_call(
        functools.partial(fast_kernel, n),
        out_shape=[
            jax.ShapeDtypeStruct((OWN, BS, BS), jnp.float32),
            jax.ShapeDtypeStruct((1, 1), jnp.int32),
        ],
        in_specs=[
            pl.BlockSpec(memory_space=pl.ANY),
            pl.BlockSpec(memory_space=pltpu.VMEM),
            pl.BlockSpec(memory_space=pltpu.SMEM),
        ],
        out_specs=[
            pl.BlockSpec(memory_space=pl.ANY),
            pl.BlockSpec(memory_space=pltpu.SMEM),
        ],
        scratch_shapes=[
            buffer(OWN),
            buffer(OWN),
            buffer(OWN),
            buffer(OWN),
            buffer(CAP),
            buffer(OWN),
            buffer(CAP),
            half,
            half,
            pltpu.VMEM((RB, BS, NNZ * BS), jnp.float32),
            pltpu.VMEM((BS, NNZ * BS), jnp.bfloat16),
            pltpu.VMEM((BS, NNZ * BS), jnp.bfloat16),
            pltpu.VMEM((8, 128), jnp.int32),
            pltpu.VMEM((SLOTS, 8, 128), jnp.int32),
            pltpu.VMEM((16, 128), jnp.int32),
            pltpu.VMEM((2, 16, 128), jnp.int32),
            pltpu.VMEM((rows, 128), jnp.int32),
            pltpu.SMEM((rows, 128), jnp.int32),
            pltpu.VMEM((TROWS, 128), jnp.int32),
            pltpu.SMEM((TROWS, 128), jnp.int32),
            pltpu.SMEM((OWN * NNZ,), jnp.int32),
            pltpu.VMEM((ROUNDS + 1, 8, 128), jnp.float32),
            pltpu.VMEM((ROUNDS, 8, 128), jnp.float32),
            pltpu.VMEM((GROUPS - 1, 8, 128), jnp.float32),
            dma((6,)),
            dma((6,)),
            dma((2,)),
            dma((2,)),
            dma((STEPS,)),
            dma((STEPS,)),
            dma((PSTEPS,)),
            dma((PSTEPS,)),
            dma((STEPS,)),
            dma((STEPS,)),
            dma((ASTEPS,)),
            dma((ASTEPS,)),
            dma((1,)),
            dma((1,)),
            dma((ROUNDS,)),
            dma((ROUNDS,)),
            dma((GROUPS - 1,)),
            dma((GROUPS - 1,)),
            dma((2 + RB,)),
        ],
        compiler_params=pltpu.CompilerParams(
            collective_id=0, has_side_effects=True, vmem_limit_bytes=58 << 20
        ),
        name="mcweeny_fast",
    )(blocks, block_cols, block_cols)


def keep_kernel(src, dst, buf, got, put):
    parts = range(KEEP)
    rows = [pl.ds(i * (OWN // KEEP), OWN // KEEP) for i in parts]
    loads = [pltpu.make_async_copy(src.at[rows[i]], buf.at[rows[i]], got.at[i]) for i in parts]
    stores = [pltpu.make_async_copy(buf.at[rows[i]], dst.at[rows[i]], put.at[i]) for i in parts]
    for load in loads:
        load.start()
    for load, store in zip(loads, stores):
        load.wait()
        store.start()
    for store in stores:
        store.wait()


def keep(blocks):
    dma = pltpu.SemaphoreType.DMA
    return pl.pallas_call(
        keep_kernel,
        out_shape=jax.ShapeDtypeStruct(blocks.shape, blocks.dtype),
        in_specs=[pl.BlockSpec(memory_space=pl.ANY)],
        out_specs=pl.BlockSpec(memory_space=pl.ANY),
        scratch_shapes=[
            pltpu.VMEM((OWN, BS, BS), jnp.float32),
            dma((KEEP,)),
            dma((KEEP,)),
        ],
        compiler_params=pltpu.CompilerParams(vmem_limit_bytes=58 << 20),
        name="keep",
    )(blocks)


def body(density_blocks, block_cols, n):
    blocks = density_blocks.reshape(OWN, BS, BS)
    out, over = call_fast(blocks, block_cols, n)
    out = lax.cond(
        over[0, 0] > 0,
        lambda b, c, o: call_full(b, c, n),
        lambda b, c, o: o,
        blocks,
        block_cols,
        out,
    )
    return keep(out).reshape(RB, NNZ, BS, BS)


def solution(mesh):
    placed = (P("grid", None, None, None), P("grid", None))
    return jax.shard_map(
        functools.partial(body, n=mesh.shape["grid"]),
        mesh=mesh,
        in_specs=placed,
        out_specs=P("grid", None, None, None),
        check_vma=False,
    )
```
